32 devices in a mesh: ctx: 16 (over z, y, core), tp: 2 (over x).
Axes of the slice: x: 2, y: 2, z: 4, core: 2. Of those that a mesh axis runs over, the one named last changes fastest.
Arguments:
- queries: bfloat16 [4096, 4096], P('ctx', 'tp'), may hold values from -5 to 5
- key_head_array: bfloat16 [4096, 1024], P('ctx', 'tp'), may hold values from -8 to 8
- value_head_array: bfloat16 [4096, 1024], P('ctx', 'tp'), may hold values from -6 to 6
- ssm_input: bfloat16 [4096, 4096], P('ctx', 'tp'), may hold values from -6 to 6
- ssm_gate: bfloat16 [4096, 4096], P('ctx', 'tp'), may hold values from -30 to 30
- ssm_write: bfloat16 [4096, 1024], P('ctx', 'tp'), may hold values from -2.5 to 2.5
- ssm_read: bfloat16 [4096, 1024], P('ctx', 'tp'), may hold values from -2.5 to 2.5
- step_size: float32 [64, 4096], P('tp', 'ctx'), may hold values from 0.005 to 0.1
- log_decay: float32 [64, 4096], P('tp', 'ctx'), may hold values from -1 to 0
- skip_gain: float32 [64], P('tp'), may hold values from 0.5 to 2
- norm_gain: float32 [4096], P('tp'), may hold values from 0.1 to 1.9
- out_weight: bfloat16 [4096, 2048], P('tp'), may hold values from -2 to 2
Outputs:
- attn_mixed: float32 [4096, 2048], P('ctx', 'tp')
- ssm_output: float32 [4096, 4096], P('ctx', 'tp')
The draws below stay inside these ranges and needn't reach their ends.
All inputs are finite; a program needn't handle non-finite values.
Results may differ from the reference program's by a relative error of at most 0.0053.
Values may be sent and summed in bfloat16 or wider, within the bound.
No kernel may reach another device: no remote copies, remote signals or barrier semaphores. Data moves between devices by JAX's collectives and lax.ppermute only.
A program may use at most 128 MiB of HBM per device.

```python
import math
import jax
import jax.numpy as jnp
import numpy as np
from jax import lax

QUERY_HEADS = 32
KEY_VALUE_HEADS = 8
HEAD_SIZE = 128
DW = 2048
STATE_HEADS = 64
P_SIZE = 64
NS = 128
G = 8
TOK_DEV = 256
SPAN = 128
PROMPT_LENGTH = 4096
N_CTX = 16


def draw_queries(key, part):
    own_key = jax.random.fold_in(key, 101)
    sampled_values = jnp.clip(jax.random.normal(jax.random.fold_in(own_key, 1), (PROMPT_LENGTH, QUERY_HEADS, HEAD_SIZE), jnp.float32), -4.5, 4.5)
    return sampled_values.reshape(PROMPT_LENGTH, QUERY_HEADS * HEAD_SIZE).astype(jnp.bfloat16)


def draw_key_head_array(key, part):
    own_key = jax.random.fold_in(key, 102)
    sampled_values = jnp.clip(2.0 * jax.random.normal(jax.random.fold_in(own_key, 1), (PROMPT_LENGTH, KEY_VALUE_HEADS, HEAD_SIZE), jnp.float32), -8.0, 8.0)
    return sampled_values.reshape(PROMPT_LENGTH, KEY_VALUE_HEADS * HEAD_SIZE).astype(jnp.bfloat16)


def draw_ssm_gate(key, part):
    key = jax.random.fold_in(key, 103)
    sampled_values = jnp.clip(jax.random.normal(jax.random.fold_in(key, 1), (PROMPT_LENGTH, STATE_HEADS * P_SIZE), jnp.float32), -3.3, 3.3)
    column_scale = jnp.exp(jax.random.uniform(jax.random.fold_in(key, 2), (STATE_HEADS * P_SIZE,), jnp.float32, math.log(0.3), math.log(3.0)))
    row_scale = jnp.exp(jax.random.uniform(jax.random.fold_in(key, 3), (PROMPT_LENGTH,), jnp.float32, math.log(0.3), math.log(3.0)))
    return (sampled_values * column_scale[None, :] * row_scale[:, None]).astype(jnp.bfloat16)


def draw_log_decay(key, part):
    key = jax.random.fold_in(key, 104)
    fast_share = 5
    fast = jax.random.randint(jax.random.fold_in(key, 1), (STATE_HEADS,), 0, 10) < fast_share
    fast_rate = jnp.exp(jax.random.uniform(jax.random.fold_in(key, 2), (STATE_HEADS,), jnp.float32, math.log(0.05), math.log(0.1)))
    slow_rate = jnp.exp(jax.random.uniform(jax.random.fold_in(key, 3), (STATE_HEADS,), jnp.float32, math.log(0.15), math.log(0.6))) / PROMPT_LENGTH
    head_decay_rate = jnp.where(fast, fast_rate, slow_rate)
    coarse_noise = jax.random.uniform(jax.random.fold_in(key, 4), (STATE_HEADS, PROMPT_LENGTH), jnp.float32, 0.5, 1.5)
    per_device = jnp.exp(jax.random.uniform(jax.random.fold_in(key, 5), (STATE_HEADS, PROMPT_LENGTH // TOK_DEV), jnp.float32, math.log(0.5), math.log(2.0)))
    machine_multiplier = jnp.repeat(per_device, TOK_DEV, axis=1)
    spike_position = jax.random.randint(jax.random.fold_in(key, 6), (STATE_HEADS, 2), 0, PROMPT_LENGTH)
    spike_amplitude = jnp.any(jnp.arange(PROMPT_LENGTH, dtype=jnp.int32)[None, None, :] == spike_position[:, :, None], axis=1)
    spike_falloff = jnp.log(jax.random.uniform(jax.random.fold_in(key, 7), (STATE_HEADS, PROMPT_LENGTH), jnp.float32, 0.5, 0.8))
    return jnp.where(spike_amplitude, spike_falloff, 0.0) - head_decay_rate[:, None] * coarse_noise * machine_multiplier


def level_of(key, extent, cuts, smallest, top_value):
    def one(dim, shards_of):
        heights = jax.random.uniform(jax.random.fold_in(jax.random.fold_in(key, 6), dim), (shards_of,), jnp.float32, smallest / len(cuts), top_value / len(cuts))
        return jnp.repeat(jnp.exp(heights), extent[dim] // shards_of).reshape((-1,) + (1,) * (len(extent) - dim - 1))

    gain = one(*cuts[0])
    for cut in cuts[1:]:
        gain = gain * one(*cut)
    return gain


def normal_values(rng, extent, scale, reach, cuts=(), kind=jnp.bfloat16):
    drawn = jax.random.normal(rng, extent, jnp.float32) * scale
    if len(cuts) > 0:
        drawn = level_of(rng, extent, cuts, -0.22, 0.18) * drawn
    return jnp.clip(drawn, min=-reach, max=reach).astype(kind)


def setup_inputs(seed: int = 0) -> dict:
    key_list = jax.random.split(jax.random.key(seed), 13)
    return {
        "queries": draw_queries(jax.random.fold_in(key_list[12], 71), 0),
        "key_head_array": draw_key_head_array(jax.random.fold_in(key_list[12], 71), 0),
        "value_head_array": normal_values(key_list[2], (PROMPT_LENGTH, KEY_VALUE_HEADS * HEAD_SIZE), 1.0, 6.0, ((0, 16), (1, 2))),
        "ssm_input": normal_values(key_list[3], (PROMPT_LENGTH, STATE_HEADS * P_SIZE), 1.0, 6.0, ((0, 16), (1, 2))),
        "ssm_gate": draw_ssm_gate(jax.random.fold_in(key_list[12], 71), 0),
        "ssm_write": normal_values(key_list[5], (PROMPT_LENGTH, G * NS), 0.4, 2.5, ((0, 16), (1, 2))),
        "ssm_read": normal_values(key_list[6], (PROMPT_LENGTH, G * NS), 0.4, 2.5, ((0, 16), (1, 2))),
        "step_size": jnp.clip(jnp.exp(math.log(0.1) - 2.9957323 * jax.random.uniform(key_list[7], (STATE_HEADS, PROMPT_LENGTH), jnp.float32) ** level_of(key_list[7], (STATE_HEADS, PROMPT_LENGTH), ((0, 2), (1, 16)), -0.2, 0.2)), 0.005, 0.1),
        "log_decay": draw_log_decay(jax.random.fold_in(key_list[12], 71), 0),
        "skip_gain": jnp.clip(0.5 + 1.5 * jax.random.uniform(key_list[9], (STATE_HEADS,), jnp.float32) ** level_of(key_list[9], (STATE_HEADS,), ((0, 2),), -0.2, 0.2), 0.5, 2.0),
        "norm_gain": jnp.clip(1.0 + 0.18 * jax.random.normal(key_list[10], (STATE_HEADS * P_SIZE,), jnp.float32), 0.1, 1.9),
        "out_weight": normal_values(key_list[11], (QUERY_HEADS * HEAD_SIZE, DW), 0.125, 2.0, ((0, 2),)),
    }


def fold_tables():
    blocks = 2 * N_CTX
    block_order = np.array([index // 2 if index % 2 == 0 else blocks - 1 - index // 2 for index in range(blocks)], dtype=np.int32)
    inverse_order = np.argsort(block_order).astype(np.int32)
    return (jnp.asarray(block_order, dtype=jnp.int32), jnp.asarray(inverse_order, dtype=jnp.int32))

def regroup(values_in, along, table):
    full_shape = values_in.shape
    split_shape = full_shape[:along] + (2 * N_CTX, SPAN) + full_shape[along + 1:]
    return jnp.take(values_in.reshape(split_shape), table, axis=along).reshape(full_shape)

def restore_natural_order(values_in, along):
    return regroup(values_in, along, fold_tables()[1])

def to_folded(values_in, along):
    return regroup(values_in, along, fold_tables()[0])

def attend_group(query_group, key_one, value_one):
    rows_each = math.gcd(512, PROMPT_LENGTH)
    score_scale = 1.0 / math.sqrt(HEAD_SIZE)
    key_pos = jnp.arange(PROMPT_LENGTH, dtype=jnp.int32)

    def one_head(query_one):

        def one_block(block_index):
            start_row = block_index * rows_each
            query_rows = lax.dynamic_slice_in_dim(query_one, start_row, rows_each, 0)
            query_pos = start_row + jnp.arange(rows_each, dtype=jnp.int32)
            scores = jnp.dot(query_rows, key_one.T, preferred_element_type=jnp.float32) * score_scale
            allowed = key_pos[None, :] <= query_pos[:, None]
            row_top = lax.optimization_barrier(jnp.max(jnp.where(allowed, scores, -jnp.inf), axis=1, keepdims=True))
            weights = jnp.where(allowed, jnp.exp(scores - row_top), 0.0)
            row_total = lax.optimization_barrier(jnp.sum(weights, axis=1, keepdims=True))
            mixed_rows = jnp.dot(weights.astype(jnp.bfloat16), value_one, preferred_element_type=jnp.float32)
            return (mixed_rows / row_total).astype(jnp.bfloat16)
        pieces = lax.map(one_block, jnp.arange(PROMPT_LENGTH // rows_each, dtype=jnp.int32))
        return pieces.reshape(PROMPT_LENGTH, HEAD_SIZE)
    return lax.map(one_head, query_group)

def reference(queries, key_head_array, value_head_array, ssm_input, ssm_gate, ssm_write, ssm_read, step_size, log_decay, skip_gain, norm_gain, out_weight):
    group_repeat = QUERY_HEADS // KEY_VALUE_HEADS
    query_natural_order = restore_natural_order(queries, 0).reshape(PROMPT_LENGTH, KEY_VALUE_HEADS, group_repeat, HEAD_SIZE).transpose(1, 2, 0, 3)
    key_natural_order = restore_natural_order(key_head_array, 0).reshape(PROMPT_LENGTH, KEY_VALUE_HEADS, HEAD_SIZE).transpose(1, 0, 2)
    value_natural_order = restore_natural_order(value_head_array, 0).reshape(PROMPT_LENGTH, KEY_VALUE_HEADS, HEAD_SIZE).transpose(1, 0, 2)
    heads_out = lax.map(lambda grouped: attend_group(grouped[0], grouped[1], grouped[2]), (query_natural_order, key_natural_order, value_natural_order))
    attn_heads = heads_out.transpose(2, 0, 1, 3).reshape(PROMPT_LENGTH, QUERY_HEADS * HEAD_SIZE)
    attn_mixed = jnp.dot(attn_heads, out_weight, preferred_element_type=jnp.float32)
    attn_mixed = to_folded(attn_mixed, 0)
    per_group = STATE_HEADS // G
    blocks = 2 * N_CTX
    input_all = restore_natural_order(ssm_input, 0).reshape(blocks, SPAN, G, per_group, P_SIZE)
    gate_all = restore_natural_order(ssm_gate, 0).reshape(blocks, SPAN, G, per_group * P_SIZE)
    write_all = restore_natural_order(ssm_write, 0).reshape(blocks, SPAN, G, NS)
    read_all = restore_natural_order(ssm_read, 0).reshape(blocks, SPAN, G, NS)
    step_all = restore_natural_order(step_size, 1).reshape(G, per_group, blocks, SPAN).transpose(2, 0, 1, 3)
    decay_all = restore_natural_order(log_decay, 1).reshape(G, per_group, blocks, SPAN).transpose(2, 0, 1, 3)
    skip_cols = skip_gain.reshape(G, per_group)
    gain_cols = norm_gain.reshape(G, per_group * P_SIZE)
    row_ids = jnp.arange(SPAN, dtype=jnp.int32)
    causal = row_ids[:, None] >= row_ids[None, :]

    def ssm_block(entering, inputs):
        input_blk, gate_blk, write_blk, read_blk, step_blk, decay_blk = inputs
        cum_decay = jnp.cumsum(decay_blk, axis=2)
        scaled = (input_blk.astype(jnp.float32) * jnp.transpose(step_blk, (2, 0, 1))[..., None]).astype(jnp.bfloat16)
        inner_prod = jnp.einsum('tgn,sgn->gts', read_blk.astype(jnp.float32), write_blk.astype(jnp.float32))
        decay_gap = cum_decay[..., :, None] - cum_decay[..., None, :]
        mixing = jnp.where(causal, inner_prod[:, None] * jnp.exp(jnp.where(causal, decay_gap, 0.0)), 0.0).astype(jnp.bfloat16)
        local_out = jnp.einsum('gjts,sgjp->tgjp', mixing.astype(jnp.float32), scaled.astype(jnp.float32))
        tail_decay = jnp.exp(cum_decay[..., -1:] - cum_decay)
        written = (jnp.transpose(write_blk, (1, 0, 2)).astype(jnp.float32)[:, None] * tail_decay[..., None]).astype(jnp.bfloat16)
        block_state = jnp.einsum('sgjp,gjsn->gjpn', scaled.astype(jnp.float32), written.astype(jnp.float32))
        carried = jnp.einsum('tgn,gjpn->tgjp', read_blk.astype(jnp.float32), entering, precision=lax.Precision.HIGHEST)
        mixed_out = local_out + carried * jnp.transpose(jnp.exp(cum_decay), (2, 0, 1))[..., None] + skip_cols[None, :, :, None] * input_blk.astype(jnp.float32)
        gated = mixed_out.reshape(SPAN, G, per_group * P_SIZE) * jax.nn.silu(gate_blk.astype(jnp.float32))
        mean_square = lax.optimization_barrier(jnp.mean(gated * gated, axis=-1, keepdims=True))
        normed = gated * lax.rsqrt(mean_square + 1e-05) * gain_cols[None]
        leaving = jnp.exp(cum_decay[..., -1])[..., None, None] * entering + block_state
        return (leaving, normed.reshape(SPAN, STATE_HEADS * P_SIZE))
    start_state = jnp.zeros((G, per_group, P_SIZE, NS), jnp.float32)
    final_state, outputs = lax.scan(ssm_block, start_state, (input_all, gate_all, write_all, read_all, step_all, decay_all))
    ssm_output = to_folded(outputs.reshape(PROMPT_LENGTH, STATE_HEADS * P_SIZE), 0)
    return (attn_mixed, ssm_output)
```

```python
import functools
import math

import jax
import jax.numpy as jnp
from jax import lax
from jax.experimental import pallas as pl
from jax.experimental.pallas import tpu as pltpu
from jax.sharding import PartitionSpec as P

HEAD_SIZE = 128
P_SIZE = 64
NS = 128


neg_big = -1e30


def prefix_2(x, axis, combine, identity, reverse):
    count, mine = (lax.axis_size(axis), lax.axis_index(axis))
    everything = jax.tree.map(lambda part: lax.all_gather(part, axis), x)
    start = jax.tree.map(
        lambda part, zero: jnp.broadcast_to(jnp.asarray(zero, part.dtype), part.shape), x, identity
    )

    def lap(k, before):
        at = count - 1 - k if reverse else k
        reached = at > mine if reverse else at < mine
        new = combine(before, jax.tree.map(lambda part: part[at], everything))
        return jax.tree.map(lambda a, b: jnp.where(reached, a, b), new, before)

    return lax.fori_loop(0, count, lap, start)


def broadcast(x, axis, root):
    mine = lax.axis_index(axis) == root
    return lax.psum(jnp.where(mine, x, jnp.zeros_like(x)), axis)


def online_update(running, query_blk, key_blk, value_blk, query_pos, key_pos, score_scale):
    top_old, total_old, acc_old = running
    scores = (
        jnp.einsum("qgrd,kgd->grqk", query_blk, key_blk, preferred_element_type=jnp.float32)
        * score_scale
    )
    allowed = key_pos[None, None, None, :] <= query_pos[None, None, :, None]
    top_block = jnp.max(jnp.where(allowed, scores, neg_big), axis=-1)
    top_new = jnp.maximum(top_old, top_block)
    weights = jnp.where(allowed, jnp.exp(scores - top_new[..., None]), 0.0)
    factor = jnp.exp(top_old - top_new)
    total_new = total_old * factor + jnp.sum(weights, axis=-1)
    acc_new = acc_old * factor[..., None] + jnp.einsum(
        "grqk,kgd->grqd",
        weights.astype(jnp.bfloat16),
        value_blk,
        preferred_element_type=jnp.float32,
    )
    return (top_new, total_new, acc_new)


def compose(earlier, later):
    return (earlier[0] * later[0], later[0][..., None, None] * earlier[1] + later[1])


def steps_for():
    return 4


def body(
    queries,
    key_head_array,
    value_head_array,
    ssm_input,
    ssm_gate,
    ssm_write,
    ssm_read,
    step_size,
    log_decay,
    skip_gain,
    norm_gain,
    out_weight,
):
    ctx_count = lax.axis_size("ctx")
    ctx_index = lax.axis_index("ctx")
    tok_dev = queries.shape[0]
    half = tok_dev // 2
    kv_dev = key_head_array.shape[1] // HEAD_SIZE
    heads_dev = queries.shape[1] // HEAD_SIZE
    group_repeat = heads_dev // kv_dev
    score_scale = 1.0 / math.sqrt(HEAD_SIZE)
    last_block = 2 * ctx_count - 1
    row_ids = jnp.arange(half, dtype=jnp.int32)
    early_qpos = ctx_index * half + row_ids
    late_qpos = (last_block - ctx_index) * half + row_ids
    query_early = queries[:half].reshape(half, kv_dev, group_repeat, HEAD_SIZE)
    query_late = queries[half:].reshape(half, kv_dev, group_repeat, HEAD_SIZE)

    def fresh_state():
        return (
            jnp.full((kv_dev, group_repeat, half), neg_big, jnp.float32),
            jnp.zeros((kv_dev, group_repeat, half), jnp.float32),
            jnp.zeros((kv_dev, group_repeat, half, HEAD_SIZE), jnp.float32),
        )

    key_piece = lax.all_gather(key_head_array, "ctx", axis=0, tiled=True)
    value_piece = lax.all_gather(value_head_array, "ctx", axis=0, tiled=True)
    shard_count = key_piece.shape[0] // tok_dev
    per_step = steps_for()
    turns = shard_count // per_step
    key_groups = key_piece.reshape(turns, per_step, 2, half, kv_dev, HEAD_SIZE)
    value_groups = value_piece.reshape(turns, per_step, 2, half, kv_dev, HEAD_SIZE)

    def one_turn(running_pair, inputs):
        key_grp, value_grp, turn_index = inputs
        base_shard = turn_index * per_step
        shard_ids = base_shard + jnp.arange(per_step, dtype=jnp.int32)
        early_kpos = (shard_ids[:, None] * half + row_ids[None, :]).reshape(-1)
        late_kpos = ((last_block - shard_ids)[:, None] * half + row_ids[None, :]).reshape(-1)
        early_keys = key_grp[:, 0].reshape(per_step * half, kv_dev, HEAD_SIZE)
        late_keys = key_grp[:, 1].reshape(per_step * half, kv_dev, HEAD_SIZE)
        early_vals = value_grp[:, 0].reshape(per_step * half, kv_dev, HEAD_SIZE)
        late_vals = value_grp[:, 1].reshape(per_step * half, kv_dev, HEAD_SIZE)
        run_early, run_late = running_pair
        run_early = lax.cond(
            base_shard <= ctx_index,
            lambda running_now: online_update(
                running_now,
                query_early,
                early_keys,
                early_vals,
                early_qpos,
                early_kpos,
                score_scale,
            ),
            lambda running_now: running_now,
            run_early,
        )
        run_late = online_update(
            run_late, query_late, early_keys, early_vals, late_qpos, early_kpos, score_scale
        )
        run_late = lax.cond(
            base_shard + per_step - 1 >= ctx_index,
            lambda running_now: online_update(
                running_now, query_late, late_keys, late_vals, late_qpos, late_kpos, score_scale
            ),
            lambda running_now: running_now,
            run_late,
        )
        return ((run_early, run_late), None)

    result_pair, unused_out = lax.scan(
        one_turn,
        (fresh_state(), fresh_state()),
        (key_groups, value_groups, jnp.arange(turns, dtype=jnp.int32)),
    )

    def finish(running):
        top_fin, total_fin, acc_fin = running
        heads_out = acc_fin / total_fin[..., None]
        return (
            jnp.transpose(heads_out, (2, 0, 1, 3))
            .reshape(half, heads_dev * HEAD_SIZE)
            .astype(jnp.bfloat16)
        )

    attn_heads = jnp.concatenate([finish(result_pair[0]), finish(result_pair[1])], axis=0)
    head_terms = jnp.dot(attn_heads, out_weight, preferred_element_type=jnp.float32)
    attn_mixed = lax.psum_scatter(head_terms, "tp", scatter_dimension=1, tiled=True)
    heads_ssm = step_size.shape[0]
    groups_dev = ssm_write.shape[1] // NS
    per_group = heads_ssm // groups_dev
    causal = row_ids[:, None] >= row_ids[None, :]
    skip_cols = skip_gain.reshape(groups_dev, per_group)
    gain_cols = norm_gain.reshape(groups_dev, per_group * P_SIZE)

    def block_parts(row_from):
        cum_decay = jnp.dot(
            log_decay[:, row_from : row_from + half],
            (row_ids[:, None] <= row_ids[None, :]).astype(jnp.float32),
            precision=lax.Precision.HIGHEST,
        ).reshape(groups_dev, per_group, half)
        step_blk = step_size[:, row_from : row_from + half].reshape(groups_dev, per_group, half)
        input_blk = ssm_input[row_from : row_from + half].reshape(
            half, groups_dev, per_group, P_SIZE
        )
        write_blk = ssm_write[row_from : row_from + half].reshape(half, groups_dev, NS)
        read_blk = ssm_read[row_from : row_from + half].reshape(half, groups_dev, NS)
        scaled = (
            input_blk.astype(jnp.float32) * jnp.transpose(step_blk, (2, 0, 1))[..., None]
        ).astype(jnp.bfloat16)
        inner_prod = jnp.einsum(
            "tgn,sgn->gts", read_blk, write_blk, preferred_element_type=jnp.float32
        )
        decay_gap = cum_decay[..., :, None] - cum_decay[..., None, :]
        mixing = jnp.where(
            causal, inner_prod[:, None] * jnp.exp(jnp.where(causal, decay_gap, 0.0)), 0.0
        ).astype(jnp.bfloat16)
        local_out = jnp.einsum(
            "gjts,sgjp->tgjp", mixing, scaled, preferred_element_type=jnp.float32
        )
        tail_decay = jnp.exp(cum_decay[..., -1:] - cum_decay)
        written = (
            jnp.transpose(write_blk, (1, 0, 2)).astype(jnp.float32)[:, None] * tail_decay[..., None]
        ).astype(jnp.bfloat16)
        block_state = jnp.einsum(
            "sgjp,gjsn->gjpn", scaled, written, preferred_element_type=jnp.float32
        )
        block_decay = jnp.exp(cum_decay[..., -1])
        return ((block_decay, block_state), (local_out, cum_decay, read_blk, input_blk, row_from))

    def block_output(entering, pieces):
        local_out, cum_decay, read_blk, input_blk, row_from = pieces
        carried = jnp.einsum(
            "tgn,gjpn->tgjp",
            read_blk.astype(jnp.float32),
            entering,
            precision=lax.Precision.HIGHEST,
        )
        mixed_out = (
            local_out
            + carried * jnp.transpose(jnp.exp(cum_decay), (2, 0, 1))[..., None]
            + skip_cols[None, :, :, None] * input_blk.astype(jnp.float32)
        )
        gate_blk = ssm_gate[row_from : row_from + half].reshape(
            half, groups_dev, per_group * P_SIZE
        )
        gated = mixed_out.reshape(half, groups_dev, per_group * P_SIZE) * jax.nn.silu(
            gate_blk.astype(jnp.float32)
        )
        mean_square = jnp.mean(gated * gated, axis=-1, keepdims=True)
        normed = gated * lax.rsqrt(mean_square + 1e-05) * gain_cols[None]
        return normed.reshape(half, heads_ssm * P_SIZE)

    early_elem, early_rest = block_parts(0)
    late_elem, late_rest = block_parts(half)
    unit_decay = jnp.ones((groups_dev, per_group), jnp.float32)
    zero_state = jnp.zeros((groups_dev, per_group, P_SIZE, NS), jnp.float32)
    prefix = prefix_2(
        (early_elem[0], early_elem[1]), "ctx", compose, (unit_decay, zero_state), False
    )
    inclusive = compose(prefix, early_elem)
    total_state = broadcast(inclusive[1], "ctx", ctx_count - 1)
    suffix = prefix_2((late_elem[0], late_elem[1]), "ctx", compose, (unit_decay, zero_state), True)
    late_entering = suffix[0][..., None, None] * total_state + suffix[1]
    ssm_output = jnp.concatenate(
        [block_output(prefix[1], early_rest), block_output(late_entering, late_rest)], axis=0
    )
    return (attn_mixed, ssm_output)


LOG2E = 1.4426950408889634
F32 = jnp.float32
BF16 = jnp.bfloat16
HIGH = lax.Precision.HIGHEST
NT = (((1,), (1,)), ((), ()))
TN = (((0,), (0,)), ((), ()))
VMEM_SPEC = pl.BlockSpec(memory_space=pltpu.VMEM)


def expand_pairs(cols, pair):
    rows = cols.shape[0]
    lane = lax.broadcasted_iota(jnp.int32, (rows, 2 * P_SIZE), 1)
    first, second = cols[:, 2 * pair : 2 * pair + 1], cols[:, 2 * pair + 1 : 2 * pair + 2]
    return jnp.where(lane < P_SIZE, first, second)


def ssm_local_kernel(x_ref, write_ref, read_ref, step_ref, ldc_ref, ldr_ref, skip_ref, mixed_ref, state_ref):
    span = x_ref.shape[0]
    per_group = step_ref.shape[2]
    row = lax.broadcasted_iota(jnp.int32, (span, span), 0)
    col = lax.broadcasted_iota(jnp.int32, (span, span), 1)
    causal = col <= row
    tri = causal.astype(F32)
    ldc, ldr, step = ldc_ref[0], ldr_ref[0], step_ref[0]
    cum_c = jnp.dot(tri, ldc, precision=HIGH, preferred_element_type=F32)
    cum_r = lax.dot_general(ldr, tri, NT, precision=HIGH, preferred_element_type=F32)
    write, read = write_ref[...], read_ref[...]
    inner = lax.dot_general(read, write, NT, preferred_element_type=F32)
    last = cum_c[span - 1 : span, :]
    tail = jnp.exp(last - cum_c)
    lane = lax.broadcasted_iota(jnp.int32, (span, 2 * P_SIZE), 1)
    weighted = []
    for pair in range(per_group // 2):
        cols = pl.ds(pair * 2 * P_SIZE, 2 * P_SIZE)
        x = x_ref[:, cols].astype(F32)
        scaled = (x * expand_pairs(step, pair)).astype(BF16)
        mixes = []
        for head in (2 * pair, 2 * pair + 1):
            gap = cum_c[:, head : head + 1] - cum_r[head : head + 1, :]
            decay = jnp.exp(jnp.where(causal, gap, 0.0))
            mixes.append(jnp.where(causal, inner * decay, 0.0).astype(BF16))
        zero = jnp.zeros_like(scaled)
        stacked = jnp.concatenate(
            [jnp.where(lane < P_SIZE, scaled, zero), jnp.where(lane >= P_SIZE, scaled, zero)], axis=0
        )
        local = jnp.dot(jnp.concatenate(mixes, axis=1), stacked, preferred_element_type=F32)
        mixed_ref[:, cols] = local + skip_ref[0, :, cols] * x
        weighted.append((scaled.astype(F32) * expand_pairs(tail, pair)).astype(BF16))
        state_ref[0, pl.ds(NS, 8), cols] = jnp.broadcast_to(expand_pairs(last, pair), (8, 2 * P_SIZE))
    state_ref[0, pl.ds(0, NS), :] = lax.dot_general(
        write, jnp.concatenate(weighted, axis=1), TN, preferred_element_type=F32
    )


def ssm_out_kernel(mixed_ref, read_ref, ldc_ref, enter_ref, gate_ref, gain_ref, out_ref):
    span = mixed_ref.shape[0]
    row = lax.broadcasted_iota(jnp.int32, (span, span), 0)
    col = lax.broadcasted_iota(jnp.int32, (span, span), 1)
    tri = (col <= row).astype(F32)
    cum_c = jnp.dot(tri, ldc_ref[0], precision=HIGH, preferred_element_type=F32)
    grow = jnp.exp(cum_c)
    carried = jnp.dot(read_ref[...], enter_ref[0], preferred_element_type=F32)
    grown = jnp.concatenate([expand_pairs(grow, pair) for pair in range(grow.shape[1] // 2)], axis=1)
    gate = gate_ref[...].astype(F32)
    gated = (mixed_ref[...] + carried * grown) * (gate / (1.0 + jnp.exp(-gate)))
    mean_square = jnp.mean(gated * gated, axis=1, keepdims=True)
    out_ref[...] = gated * lax.rsqrt(mean_square + 1e-05) * gain_ref[0]


def attend_tile(q, keys, values_t, running, allowed):
    m_old, l_old, acc_old = running
    c = LOG2E / math.sqrt(HEAD_SIZE)
    s = lax.dot_general(keys, q, NT, preferred_element_type=F32)
    if allowed is not None:
        s = jnp.where(allowed, s, neg_big)
    m_new = jnp.max(s, axis=0, keepdims=True)
    if m_old is not None:
        m_new = jnp.maximum(m_old, m_new)
    p = jnp.exp2((s - m_new) * c)
    l_new = jnp.sum(p, axis=0, keepdims=True)
    acc_new = jnp.dot(values_t, p.astype(BF16), preferred_element_type=F32)
    if m_old is not None:
        alpha = jnp.exp2((m_old - m_new) * c)
        l_new = l_new + alpha * l_old
        acc_new = acc_new + alpha * acc_old
    return m_new, l_new, acc_new


def plane_rows(ref, which, half, span):
    return ref[:, which, :, pl.ds(half * span, span), :].reshape(4 * span, HEAD_SIZE)


def query_tile(q_ref, turn, half, head, span):
    return q_ref[turn, :, pl.ds(half * span, span), pl.ds(head * HEAD_SIZE, HEAD_SIZE)].reshape(2 * span, HEAD_SIZE)


def attn_local_kernel(place_ref, q_ref, kv_ref, *rest):
    stat_ref, acc_ref = rest[-2:]
    y, core = place_ref[0], place_ref[1]
    span = q_ref.shape[2] // 2
    heads = q_ref.shape[3] // HEAD_SIZE
    tile = 2 * span

    def position(shape, dim, half):
        at = lax.broadcasted_iota(jnp.int32, shape, dim)
        block = jnp.where(at < span, core, 1 - core)
        return (block if half == 0 else 1 - block) * span + at % span

    def update(half, turn, head, keys, values_t, allowed, first):
        where = pl.ds(pl.multiple_of(turn * tile, tile), tile)
        running = (None, None, None)
        if not first:
            running = (
                stat_ref[half, head, pl.ds(0, 1), where],
                stat_ref[half, head, pl.ds(1, 1), where],
                acc_ref[half, head, :, where],
            )
        running = attend_tile(query_tile(q_ref, turn, half, head, span), keys, values_t, running, allowed)
        stat_ref[half, head, pl.ds(0, 1), where] = running[0]
        stat_ref[half, head, pl.ds(1, 1), where] = running[1]
        acc_ref[half, head, :, where] = running[2]

    for half in range(2):
        allowed = position((tile, 1), 0, half) <= position((1, tile), 1, half)
        for turn in range(2):
            keys = kv_ref[turn, 0, :, pl.ds(half * span, span), :].reshape(tile, HEAD_SIZE)
            values_t = kv_ref[turn, 1, :, pl.ds(half * span, span), :].reshape(tile, HEAD_SIZE).T
            for head in range(heads):
                update(half, turn, head, keys, values_t, allowed, True)
        after = 1 - y if half == 0 else y
        keys = kv_ref[1 - after, 0, :, pl.ds(half * span, span), :].reshape(tile, HEAD_SIZE)
        values_t = kv_ref[1 - after, 1, :, pl.ds(half * span, span), :].reshape(tile, HEAD_SIZE).T
        for head in range(heads):
            update(half, after, head, keys, values_t, None, False)
    keys, values_t = plane_rows(kv_ref, 0, 0, span), plane_rows(kv_ref, 1, 0, span).T
    for turn in range(2):
        for head in range(heads):
            update(1, turn, head, keys, values_t, None, False)


def attn_remote_kernel(last, later_ref, q_ref, kv_ref, stat_in, acc_in, *rest):
    if last:
        out_ref, stat_ref, acc_ref = rest[-3:]
    else:
        stat_ref, acc_ref = rest[-2:]
    later = later_ref[0]
    span = q_ref.shape[2] // 2
    heads = q_ref.shape[3] // HEAD_SIZE
    tile = 2 * span
    stat_ref[...] = stat_in[...]
    acc_ref[...] = acc_in[...]

    def unit(half, part):
        keys, values_t = plane_rows(kv_ref, 0, part, span), plane_rows(kv_ref, 1, part, span).T
        for turn in range(2):
            where = pl.ds(turn * tile, tile)
            for head in range(heads):
                running = (
                    stat_ref[half, head, pl.ds(0, 1), where],
                    stat_ref[half, head, pl.ds(1, 1), where],
                    acc_ref[half, head, :, where],
                )
                running = attend_tile(query_tile(q_ref, turn, half, head, span), keys, values_t, running, None)
                stat_ref[half, head, pl.ds(0, 1), where] = running[0]
                stat_ref[half, head, pl.ds(1, 1), where] = running[1]
                acc_ref[half, head, :, where] = running[2]

    unit(1, 0)
    unit(later, later)
    if last:
        for half in range(2):
            for head in range(heads):
                scaled = acc_ref[half, head] / stat_ref[half, head, pl.ds(1, 1), :]
                out_ref[:, :, pl.ds(half * span, span), pl.ds(head * HEAD_SIZE, HEAD_SIZE)] = scaled.T.reshape(
                    2, 2, span, HEAD_SIZE
                )


def pack(state, log_row):
    hi = lax.reduce_precision(log_row, 8, 7)
    mid = lax.reduce_precision(log_row - hi, 8, 7)
    row = lax.broadcasted_iota(jnp.int32, (16, state.shape[1]), 0)
    rest = jnp.where(row == 0, hi, jnp.where(row == 1, mid, jnp.where(row == 2, log_row - hi - mid, 0.0)))
    return jnp.concatenate([state.astype(BF16), rest.astype(BF16)], axis=0)


def unpack(packed):
    return packed[:NS].astype(F32), jnp.sum(packed[NS:].astype(F32), axis=0, keepdims=True)


def chain(first, second):
    return jnp.exp(second[1]) * first[0] + second[0], first[1] + second[1]


def split_body(
    queries,
    key_head_array,
    value_head_array,
    ssm_input,
    ssm_gate,
    ssm_write,
    ssm_read,
    step_size,
    log_decay,
    skip_gain,
    norm_gain,
    out_weight,
):
    planes = lax.axis_size("ctx") // 4
    ctx_index = lax.axis_index("ctx")
    tp_index = lax.axis_index("tp")
    z, y, core = ctx_index // 4, (ctx_index // 2) % 2, ctx_index % 2
    tok_dev = queries.shape[0]
    half = tok_dev // 2
    group = queries.shape[1] // 4
    everyone = range(4 * planes)
    to_core = [(i, i ^ 1) for i in everyone]
    to_y = [(i, i ^ 2) for i in everyone]

    def send(x, pairs):
        return lax.ppermute(x, "ctx", pairs)

    def part(x, which, width, axis):
        return lax.dynamic_slice_in_dim(x, which * width, width, axis)

    def in_order(mine, other, at, axis=0):
        return jnp.concatenate([jnp.where(at == 0, mine, other), jnp.where(at == 0, other, mine)], axis=axis)

    def both(which):
        return jnp.stack(
            [part(key_head_array, which, 2 * HEAD_SIZE, 1), part(value_head_array, which, 2 * HEAD_SIZE, 1)]
        )

    kv_chip = jnp.stack([both(core), send(both(1 - core), to_core)], axis=1)
    kv_own = jnp.stack(
        [part(kv_chip, y, HEAD_SIZE, 3), send(part(kv_chip, 1 - y, HEAD_SIZE, 3), to_y)]
    )
    kv_from = [
        send(kv_own, [(i, (i + 4 * turn) % (4 * planes)) for i in everyone]) for turn in range(1, planes)
    ]

    q_chip = jnp.stack([part(queries, core, 2 * group, 1), send(part(queries, 1 - core, 2 * group, 1), to_core)])
    q_own = jnp.stack([part(q_chip, y, group, 2), send(part(q_chip, 1 - y, group, 2), to_y)])

    groups = ssm_write.shape[1] // NS
    per_group = step_size.shape[0] // groups
    width = per_group * P_SIZE
    by_group = (groups, per_group, tok_dev)
    step_cols = jnp.transpose(step_size.reshape(by_group), (0, 2, 1))
    ld_rows = log_decay.reshape(by_group)
    ld_cols = jnp.transpose(ld_rows, (0, 2, 1))
    skip_rows = jnp.repeat(skip_gain, P_SIZE).reshape(groups, 1, width)
    gain_rows = norm_gain.reshape(groups, 1, width)
    wide = pl.BlockSpec((half, width), lambda b, g: (b, g))
    narrow = pl.BlockSpec((half, NS), lambda b, g: (b, g))
    columns = pl.BlockSpec((1, half, per_group), lambda b, g: (g, b, 0))
    per_row = pl.BlockSpec((1, 1, width), lambda b, g: (g, 0, 0))
    mixed, states = pl.pallas_call(
        ssm_local_kernel,
        grid=(2, groups),
        in_specs=[
            wide,
            narrow,
            narrow,
            columns,
            columns,
            pl.BlockSpec((1, per_group, half), lambda b, g: (g, 0, b)),
            per_row,
        ],
        out_specs=[wide, pl.BlockSpec((1, NS + 8, width), lambda b, g: (b, 0, g))],
        out_shape=[
            jax.ShapeDtypeStruct((tok_dev, groups * width), F32),
            jax.ShapeDtypeStruct((2, NS + 8, groups * width), F32),
        ],
        compiler_params=pltpu.CompilerParams(vmem_limit_bytes=32 * 2**20),
        cost_estimate=pl.CostEstimate(flops=4 * 10**8, bytes_accessed=6 * 2**20, transcendentals=10**6),
        name="ssm_local",
    )(ssm_input, ssm_write, ssm_read, step_cols, ld_cols, ld_rows, skip_rows)

    st_mine = part(states, core, 2 * width, 2)
    st_other = send(part(states, 1 - core, 2 * width, 2), to_core)
    st_zero, st_one = jnp.where(core == 0, st_mine, st_other), jnp.where(core == 0, st_other, st_mine)

    def elem(packed):
        return packed[:NS], packed[NS : NS + 1]

    early_chip = chain(elem(st_zero[0]), elem(st_one[0]))
    late_chip = chain(elem(st_one[1]), elem(st_zero[1]))
    chip_pack = jnp.stack([pack(*early_chip), pack(*late_chip)])
    cp_mine = part(chip_pack, y, width, 2)
    cp_other = send(part(chip_pack, 1 - y, width, 2), to_y)
    cp_zero, cp_one = jnp.where(y == 0, cp_mine, cp_other), jnp.where(y == 0, cp_other, cp_mine)
    early_plane = chain(unpack(cp_zero[0]), unpack(cp_one[0]))
    late_plane = chain(unpack(cp_one[1]), unpack(cp_zero[1]))
    plane_pack = jnp.stack([pack(*early_plane), pack(*late_plane)])
    plane_from = jnp.stack(
        [plane_pack]
        + [send(plane_pack, [(i, (i + 4 * turn) % (4 * planes)) for i in everyone]) for turn in range(1, planes)]
    )

    def of_plane(at):
        return lax.dynamic_index_in_dim(plane_from, (z - at) % planes, 0, keepdims=False)

    total = (jnp.zeros((NS, width), F32), jnp.zeros((1, width), F32))
    enter_early = total[0]
    for at in range(planes):
        enter_early = jnp.where(z == at, total[0], enter_early)
        total = chain(total, unpack(of_plane(at)[0]))
    enter_late = total[0]
    for at in range(planes - 1, -1, -1):
        enter_late = jnp.where(z == at, total[0], enter_late)
        total = chain(total, unpack(of_plane(at)[1]))

    def step_on(state, packed):
        block = unpack(packed)
        return jnp.exp(block[1]) * state + block[0]

    early_at = [enter_early, step_on(enter_early, cp_zero[0])]
    late_at = [step_on(enter_late, cp_one[1]), enter_late]
    chip_enter = [jnp.stack([early_at[k], late_at[k]]).astype(BF16) for k in range(2)]
    ce_mine = jnp.where(y == 0, chip_enter[0], chip_enter[1])
    ce_other = send(jnp.where(y == 0, chip_enter[1], chip_enter[0]), to_y)
    ce = in_order(ce_mine, ce_other, y, axis=2).astype(F32)

    def step_by(state, block):
        return jnp.exp(block[1]) * state + block[0]

    early_block = [ce[0], step_by(ce[0], elem(st_zero[0]))]
    late_block = [step_by(ce[1], elem(st_one[1])), ce[1]]
    block_enter = [jnp.stack([early_block[k], late_block[k]]).astype(BF16) for k in range(2)]
    be_mine = jnp.where(core == 0, block_enter[0], block_enter[1])
    be_other = send(jnp.where(core == 0, block_enter[1], block_enter[0]), to_core)
    enter = in_order(be_mine, be_other, core, axis=2)

    ssm_output = pl.pallas_call(
        ssm_out_kernel,
        grid=(2, groups),
        in_specs=[
            wide,
            narrow,
            columns,
            pl.BlockSpec((1, NS, width), lambda b, g: (b, 0, g)),
            wide,
            per_row,
        ],
        out_specs=wide,
        out_shape=jax.ShapeDtypeStruct((tok_dev, groups * width), F32),
        compiler_params=pltpu.CompilerParams(vmem_limit_bytes=32 * 2**20),
        cost_estimate=pl.CostEstimate(flops=10**8, bytes_accessed=6 * 2**20, transcendentals=10**6),
        name="ssm_out",
    )(mixed, ssm_read, ld_cols, enter, ssm_gate, gain_rows)

    heads_own = group // HEAD_SIZE
    rows = 4 * half
    stat_shape = jax.ShapeDtypeStruct((2, heads_own, 8, rows), F32)
    acc_shape = jax.ShapeDtypeStruct((2, heads_own, HEAD_SIZE, rows), F32)
    params = pltpu.CompilerParams(vmem_limit_bytes=40 * 2**20)
    cost = pl.CostEstimate(flops=2 * 10**9, bytes_accessed=8 * 2**20, transcendentals=2 * 10**6)
    smem = pl.BlockSpec(memory_space=pltpu.SMEM)
    anywhere = pl.BlockSpec(memory_space=pl.ANY)
    after_local = [st_other]
    stat, acc = pl.pallas_call(
        attn_local_kernel,
        in_specs=[smem] + [VMEM_SPEC] * 2 + [anywhere] * len(after_local),
        out_specs=[VMEM_SPEC] * 2,
        out_shape=[stat_shape, acc_shape],
        compiler_params=params,
        cost_estimate=cost,
        name="attn_local",
    )(jnp.stack([y, core]).astype(jnp.int32), q_own, kv_own, *after_local)
    after_turn = {1: [cp_other], 2: [], 3: []}
    for turn in range(1, planes):
        last = turn == planes - 1
        later = (z < turn).astype(jnp.int32).reshape(1)
        outs = [stat_shape, acc_shape]
        if last:
            outs = [jax.ShapeDtypeStruct(q_own.shape, F32)] + outs
        after = after_turn.get(turn, [])
        *result, stat, acc = pl.pallas_call(
            functools.partial(attn_remote_kernel, last),
            in_specs=[smem] + [VMEM_SPEC] * 4 + [anywhere] * len(after),
            out_specs=[VMEM_SPEC] * len(outs),
            out_shape=outs,
            compiler_params=params,
            cost_estimate=cost,
            name="attn_remote",
        )(later, q_own, kv_from[turn - 1], stat, acc, *after)
    heads_plane = result[0].astype(BF16)

    mine, other = heads_plane[0], send(heads_plane[1], to_y)
    chip = send(jnp.stack([mine[1], other[1]]), to_core)
    attn_heads = in_order(
        in_order(mine[0], other[0], y, axis=1), in_order(chip[0], chip[1], y, axis=1), core, axis=1
    )

    head_terms = jnp.dot(attn_heads, out_weight, preferred_element_type=F32)
    out_cols = out_weight.shape[1] // 2
    away = part(head_terms, 1 - tp_index, out_cols, 1).astype(BF16)
    came = lax.ppermute(away, "tp", [(0, 1), (1, 0)])
    attn_mixed = part(head_terms, tp_index, out_cols, 1) + came.astype(F32)
    return attn_mixed, ssm_output


def solution(mesh):
    placed = (
        P("ctx", "tp"),
        P("ctx", "tp"),
        P("ctx", "tp"),
        P("ctx", "tp"),
        P("ctx", "tp"),
        P("ctx", "tp"),
        P("ctx", "tp"),
        P("tp", "ctx"),
        P("tp", "ctx"),
        P("tp"),
        P("tp"),
        P("tp", None),
    )

    def program(*arrays):
        kv_dev, groups_dev = arrays[1].shape[1] // HEAD_SIZE, arrays[5].shape[1] // NS
        can_split = kv_dev == 4 and groups_dev == 4 and lax.axis_size("tp") == 2
        if can_split and lax.axis_size("ctx") % 4 == 0 and lax.axis_size("ctx") >= 8:
            return split_body(*arrays)
        return body(*arrays)

    return jax.shard_map(
        program,
        mesh=mesh,
        in_specs=placed,
        out_specs=(P("ctx", "tp"), P("ctx", "tp")),
        check_vma=False,
    )
```

```python
import functools
import math

import jax
import jax.numpy as jnp
from jax import lax
from jax.experimental import pallas as pl
from jax.experimental.pallas import tpu as pltpu
from jax.sharding import PartitionSpec as P

HEAD_SIZE = 128
P_SIZE = 64
NS = 128


neg_big = -1e30


def prefix_2(x, axis, combine, identity, reverse):
    count, mine = (lax.axis_size(axis), lax.axis_index(axis))
    everything = jax.tree.map(lambda part: lax.all_gather(part, axis), x)
    start = jax.tree.map(
        lambda part, zero: jnp.broadcast_to(jnp.asarray(zero, part.dtype), part.shape), x, identity
    )

    def lap(k, before):
        at = count - 1 - k if reverse else k
        reached = at > mine if reverse else at < mine
        new = combine(before, jax.tree.map(lambda part: part[at], everything))
        return jax.tree.map(lambda a, b: jnp.where(reached, a, b), new, before)

    return lax.fori_loop(0, count, lap, start)


def broadcast(x, axis, root):
    mine = lax.axis_index(axis) == root
    return lax.psum(jnp.where(mine, x, jnp.zeros_like(x)), axis)


def online_update(running, query_blk, key_blk, value_blk, query_pos, key_pos, score_scale):
    top_old, total_old, acc_old = running
    scores = (
        jnp.einsum("qgrd,kgd->grqk", query_blk, key_blk, preferred_element_type=jnp.float32)
        * score_scale
    )
    allowed = key_pos[None, None, None, :] <= query_pos[None, None, :, None]
    top_block = jnp.max(jnp.where(allowed, scores, neg_big), axis=-1)
    top_new = jnp.maximum(top_old, top_block)
    weights = jnp.where(allowed, jnp.exp(scores - top_new[..., None]), 0.0)
    factor = jnp.exp(top_old - top_new)
    total_new = total_old * factor + jnp.sum(weights, axis=-1)
    acc_new = acc_old * factor[..., None] + jnp.einsum(
        "grqk,kgd->grqd",
        weights.astype(jnp.bfloat16),
        value_blk,
        preferred_element_type=jnp.float32,
    )
    return (top_new, total_new, acc_new)


def compose(earlier, later):
    return (earlier[0] * later[0], later[0][..., None, None] * earlier[1] + later[1])


def steps_for():
    return 4


def body(
    queries,
    key_head_array,
    value_head_array,
    ssm_input,
    ssm_gate,
    ssm_write,
    ssm_read,
    step_size,
    log_decay,
    skip_gain,
    norm_gain,
    out_weight,
):
    ctx_count = lax.axis_size("ctx")
    ctx_index = lax.axis_index("ctx")
    tok_dev = queries.shape[0]
    half = tok_dev // 2
    kv_dev = key_head_array.shape[1] // HEAD_SIZE
    heads_dev = queries.shape[1] // HEAD_SIZE
    group_repeat = heads_dev // kv_dev
    score_scale = 1.0 / math.sqrt(HEAD_SIZE)
    last_block = 2 * ctx_count - 1
    row_ids = jnp.arange(half, dtype=jnp.int32)
    early_qpos = ctx_index * half + row_ids
    late_qpos = (last_block - ctx_index) * half + row_ids
    query_early = queries[:half].reshape(half, kv_dev, group_repeat, HEAD_SIZE)
    query_late = queries[half:].reshape(half, kv_dev, group_repeat, HEAD_SIZE)

    def fresh_state():
        return (
            jnp.full((kv_dev, group_repeat, half), neg_big, jnp.float32),
            jnp.zeros((kv_dev, group_repeat, half), jnp.float32),
            jnp.zeros((kv_dev, group_repeat, half, HEAD_SIZE), jnp.float32),
        )

    key_piece = lax.all_gather(key_head_array, "ctx", axis=0, tiled=True)
    value_piece = lax.all_gather(value_head_array, "ctx", axis=0, tiled=True)
    shard_count = key_piece.shape[0] // tok_dev
    per_step = steps_for()
    turns = shard_count // per_step
    key_groups = key_piece.reshape(turns, per_step, 2, half, kv_dev, HEAD_SIZE)
    value_groups = value_piece.reshape(turns, per_step, 2, half, kv_dev, HEAD_SIZE)

    def one_turn(running_pair, inputs):
        key_grp, value_grp, turn_index = inputs
        base_shard = turn_index * per_step
        shard_ids = base_shard + jnp.arange(per_step, dtype=jnp.int32)
        early_kpos = (shard_ids[:, None] * half + row_ids[None, :]).reshape(-1)
        late_kpos = ((last_block - shard_ids)[:, None] * half + row_ids[None, :]).reshape(-1)
        early_keys = key_grp[:, 0].reshape(per_step * half, kv_dev, HEAD_SIZE)
        late_keys = key_grp[:, 1].reshape(per_step * half, kv_dev, HEAD_SIZE)
        early_vals = value_grp[:, 0].reshape(per_step * half, kv_dev, HEAD_SIZE)
        late_vals = value_grp[:, 1].reshape(per_step * half, kv_dev, HEAD_SIZE)
        run_early, run_late = running_pair
        run_early = lax.cond(
            base_shard <= ctx_index,
            lambda running_now: online_update(
                running_now,
                query_early,
                early_keys,
                early_vals,
                early_qpos,
                early_kpos,
                score_scale,
            ),
            lambda running_now: running_now,
            run_early,
        )
        run_late = online_update(
            run_late, query_late, early_keys, early_vals, late_qpos, early_kpos, score_scale
        )
        run_late = lax.cond(
            base_shard + per_step - 1 >= ctx_index,
            lambda running_now: online_update(
                running_now, query_late, late_keys, late_vals, late_qpos, late_kpos, score_scale
            ),
            lambda running_now: running_now,
            run_late,
        )
        return ((run_early, run_late), None)

    result_pair, unused_out = lax.scan(
        one_turn,
        (fresh_state(), fresh_state()),
        (key_groups, value_groups, jnp.arange(turns, dtype=jnp.int32)),
    )

    def finish(running):
        top_fin, total_fin, acc_fin = running
        heads_out = acc_fin / total_fin[..., None]
        return (
            jnp.transpose(heads_out, (2, 0, 1, 3))
            .reshape(half, heads_dev * HEAD_SIZE)
            .astype(jnp.bfloat16)
        )

    attn_heads = jnp.concatenate([finish(result_pair[0]), finish(result_pair[1])], axis=0)
    head_terms = jnp.dot(attn_heads, out_weight, preferred_element_type=jnp.float32)
    attn_mixed = lax.psum_scatter(head_terms, "tp", scatter_dimension=1, tiled=True)
    heads_ssm = step_size.shape[0]
    groups_dev = ssm_write.shape[1] // NS
    per_group = heads_ssm // groups_dev
    causal = row_ids[:, None] >= row_ids[None, :]
    skip_cols = skip_gain.reshape(groups_dev, per_group)
    gain_cols = norm_gain.reshape(groups_dev, per_group * P_SIZE)

    def block_parts(row_from):
        cum_decay = jnp.dot(
            log_decay[:, row_from : row_from + half],
            (row_ids[:, None] <= row_ids[None, :]).astype(jnp.float32),
            precision=lax.Precision.HIGHEST,
        ).reshape(groups_dev, per_group, half)
        step_blk = step_size[:, row_from : row_from + half].reshape(groups_dev, per_group, half)
        input_blk = ssm_input[row_from : row_from + half].reshape(
            half, groups_dev, per_group, P_SIZE
        )
        write_blk = ssm_write[row_from : row_from + half].reshape(half, groups_dev, NS)
        read_blk = ssm_read[row_from : row_from + half].reshape(half, groups_dev, NS)
        scaled = (
            input_blk.astype(jnp.float32) * jnp.transpose(step_blk, (2, 0, 1))[..., None]
        ).astype(jnp.bfloat16)
        inner_prod = jnp.einsum(
            "tgn,sgn->gts", read_blk, write_blk, preferred_element_type=jnp.float32
        )
        decay_gap = cum_decay[..., :, None] - cum_decay[..., None, :]
        mixing = jnp.where(
            causal, inner_prod[:, None] * jnp.exp(jnp.where(causal, decay_gap, 0.0)), 0.0
        ).astype(jnp.bfloat16)
        local_out = jnp.einsum(
            "gjts,sgjp->tgjp", mixing, scaled, preferred_element_type=jnp.float32
        )
        tail_decay = jnp.exp(cum_decay[..., -1:] - cum_decay)
        written = (
            jnp.transpose(write_blk, (1, 0, 2)).astype(jnp.float32)[:, None] * tail_decay[..., None]
        ).astype(jnp.bfloat16)
        block_state = jnp.einsum(
            "sgjp,gjsn->gjpn", scaled, written, preferred_element_type=jnp.float32
        )
        block_decay = jnp.exp(cum_decay[..., -1])
        return ((block_decay, block_state), (local_out, cum_decay, read_blk, input_blk, row_from))

    def block_output(entering, pieces):
        local_out, cum_decay, read_blk, input_blk, row_from = pieces
        carried = jnp.einsum(
            "tgn,gjpn->tgjp",
            read_blk.astype(jnp.float32),
            entering,
            precision=lax.Precision.HIGHEST,
        )
        mixed_out = (
            local_out
            + carried * jnp.transpose(jnp.exp(cum_decay), (2, 0, 1))[..., None]
            + skip_cols[None, :, :, None] * input_blk.astype(jnp.float32)
        )
        gate_blk = ssm_gate[row_from : row_from + half].reshape(
            half, groups_dev, per_group * P_SIZE
        )
        gated = mixed_out.reshape(half, groups_dev, per_group * P_SIZE) * jax.nn.silu(
            gate_blk.astype(jnp.float32)
        )
        mean_square = jnp.mean(gated * gated, axis=-1, keepdims=True)
        normed = gated * lax.rsqrt(mean_square + 1e-05) * gain_cols[None]
        return normed.reshape(half, heads_ssm * P_SIZE)

    early_elem, early_rest = block_parts(0)
    late_elem, late_rest = block_parts(half)
    unit_decay = jnp.ones((groups_dev, per_group), jnp.float32)
    zero_state = jnp.zeros((groups_dev, per_group, P_SIZE, NS), jnp.float32)
    prefix = prefix_2(
        (early_elem[0], early_elem[1]), "ctx", compose, (unit_decay, zero_state), False
    )
    inclusive = compose(prefix, early_elem)
    total_state = broadcast(inclusive[1], "ctx", ctx_count - 1)
    suffix = prefix_2((late_elem[0], late_elem[1]), "ctx", compose, (unit_decay, zero_state), True)
    late_entering = suffix[0][..., None, None] * total_state + suffix[1]
    ssm_output = jnp.concatenate(
        [block_output(prefix[1], early_rest), block_output(late_entering, late_rest)], axis=0
    )
    return (attn_mixed, ssm_output)


LOG2E = 1.4426950408889634
F32 = jnp.float32
BF16 = jnp.bfloat16
HIGH = lax.Precision.HIGHEST
NT = (((1,), (1,)), ((), ()))
TN = (((0,), (0,)), ((), ()))
VMEM_SPEC = pl.BlockSpec(memory_space=pltpu.VMEM)


def expand_pairs(cols, pair):
    rows = cols.shape[0]
    lane = lax.broadcasted_iota(jnp.int32, (rows, 2 * P_SIZE), 1)
    first, second = cols[:, 2 * pair : 2 * pair + 1], cols[:, 2 * pair + 1 : 2 * pair + 2]
    return jnp.where(lane < P_SIZE, first, second)


def ssm_local_kernel(x_ref, write_ref, read_ref, step_ref, ldc_ref, ldr_ref, skip_ref, _, mixed_ref, state_ref):
    span = x_ref.shape[0]
    per_group = step_ref.shape[2]
    row = lax.broadcasted_iota(jnp.int32, (span, span), 0)
    col = lax.broadcasted_iota(jnp.int32, (span, span), 1)
    causal = col <= row
    tri = causal.astype(F32)
    ldc, ldr, step = ldc_ref[0], ldr_ref[0], step_ref[0]
    cum_c = jnp.dot(tri, ldc, precision=HIGH, preferred_element_type=F32)
    cum_r = lax.dot_general(ldr, tri, NT, precision=HIGH, preferred_element_type=F32)
    write, read = write_ref[...], read_ref[...]
    inner = lax.dot_general(read, write, NT, preferred_element_type=F32)
    last = cum_c[span - 1 : span, :]
    tail = jnp.exp(last - cum_c)
    lane = lax.broadcasted_iota(jnp.int32, (span, 2 * P_SIZE), 1)
    weighted = []
    for pair in range(per_group // 2):
        cols = pl.ds(pair * 2 * P_SIZE, 2 * P_SIZE)
        x = x_ref[:, cols].astype(F32)
        scaled = (x * expand_pairs(step, pair)).astype(BF16)
        mixes = []
        for head in (2 * pair, 2 * pair + 1):
            gap = cum_c[:, head : head + 1] - cum_r[head : head + 1, :]
            decay = jnp.exp(jnp.where(causal, gap, 0.0))
            mixes.append(jnp.where(causal, inner * decay, 0.0).astype(BF16))
        zero = jnp.zeros_like(scaled)
        stacked = jnp.concatenate(
            [jnp.where(lane < P_SIZE, scaled, zero), jnp.where(lane >= P_SIZE, scaled, zero)], axis=0
        )
        local = jnp.dot(jnp.concatenate(mixes, axis=1), stacked, preferred_element_type=F32)
        mixed_ref[:, cols] = local + skip_ref[0, :, cols] * x
        weighted.append((scaled.astype(F32) * expand_pairs(tail, pair)).astype(BF16))
        state_ref[0, pl.ds(NS, 8), cols] = jnp.broadcast_to(expand_pairs(last, pair), (8, 2 * P_SIZE))
    state_ref[0, pl.ds(0, NS), :] = lax.dot_general(
        write, jnp.concatenate(weighted, axis=1), TN, preferred_element_type=F32
    )


def ssm_out_kernel(mixed_ref, read_ref, ldc_ref, enter_ref, gate_ref, gain_ref, out_ref):
    span = mixed_ref.shape[0]
    row = lax.broadcasted_iota(jnp.int32, (span, span), 0)
    col = lax.broadcasted_iota(jnp.int32, (span, span), 1)
    tri = (col <= row).astype(F32)
    cum_c = jnp.dot(tri, ldc_ref[0], precision=HIGH, preferred_element_type=F32)
    grow = jnp.exp(cum_c)
    carried = jnp.dot(read_ref[...], enter_ref[0], preferred_element_type=F32)
    grown = jnp.concatenate([expand_pairs(grow, pair) for pair in range(grow.shape[1] // 2)], axis=1)
    gate = gate_ref[...].astype(F32)
    gated = (mixed_ref[...] + carried * grown) * (gate / (1.0 + jnp.exp(-gate)))
    mean_square = jnp.mean(gated * gated, axis=1, keepdims=True)
    out_ref[...] = gated * lax.rsqrt(mean_square + 1e-05) * gain_ref[0]


def attend_tile(q, keys, values_t, running, allowed):
    m_old, l_old, acc_old = running
    c = LOG2E / math.sqrt(HEAD_SIZE)
    s = lax.dot_general(keys, q, NT, preferred_element_type=F32)
    if allowed is not None:
        s = jnp.where(allowed, s, neg_big)
    m_new = jnp.max(s, axis=0, keepdims=True)
    if m_old is not None:
        m_new = jnp.maximum(m_old, m_new)
    p = jnp.exp2((s - m_new) * c)
    l_new = jnp.sum(p, axis=0, keepdims=True)
    acc_new = jnp.dot(values_t, p.astype(BF16), preferred_element_type=F32)
    if m_old is not None:
        alpha = jnp.exp2((m_old - m_new) * c)
        l_new = l_new + alpha * l_old
        acc_new = acc_new + alpha * acc_old
    return m_new, l_new, acc_new


def plane_rows(ref, half, which):
    chunk = ref[:, which] if half is None else ref[half, :, which]
    return chunk.reshape(-1, HEAD_SIZE)


def update_tile(q_refs, half, turn, head, keys, values_t, allowed, stat_ref, acc_ref, first):
    span = q_refs[0].shape[0] // 2
    q = jnp.concatenate(
        [
            ref[pl.ds(half * span, span), pl.ds(head * HEAD_SIZE, HEAD_SIZE)]
            for ref in q_refs[2 * turn : 2 * turn + 2]
        ],
        axis=0,
    )
    where = pl.ds(turn * 2 * span, 2 * span)
    running = (None, None, None)
    if not first:
        running = (stat_ref[head, pl.ds(0, 1), where], stat_ref[head, pl.ds(1, 1), where], acc_ref[head, :, where])
    running = attend_tile(q, keys, values_t, running, allowed)
    stat_ref[head, pl.ds(0, 1), where] = running[0]
    stat_ref[head, pl.ds(1, 1), where] = running[1]
    acc_ref[head, :, where] = running[2]


def attn_local_kernel(place_ref, *refs):
    q_refs, kv_ref, (stat_ref, acc_ref) = refs[:4], refs[4], refs[-2:]
    y, core = place_ref[0], place_ref[1]
    span = q_refs[0].shape[0] // 2
    heads = q_refs[0].shape[1] // HEAD_SIZE
    tile = 2 * span

    def position(shape, dim, half):
        at = lax.broadcasted_iota(jnp.int32, shape, dim)
        block = jnp.where(at < span, core, 1 - core)
        return (block if half == 0 else 1 - block) * span + at % span

    for half in range(2):
        state = stat_ref.at[half], acc_ref.at[half]
        allowed = position((tile, 1), 0, half) <= position((1, tile), 1, half)
        parts = []
        for turn in range(2):
            keys = kv_ref[half, 2 * turn : 2 * turn + 2, 0].reshape(tile, HEAD_SIZE)
            values_t = kv_ref[half, 2 * turn : 2 * turn + 2, 1].reshape(tile, HEAD_SIZE).T
            parts.append((keys, values_t))
            for head in range(heads):
                update_tile(q_refs, half, turn, head, keys, values_t, allowed, *state, True)
        for turn in range(2):

            @pl.when(y == (1 - turn if half == 0 else turn))
            def _():
                for head in range(heads):
                    update_tile(q_refs, half, turn, head, *parts[1 - turn], None, *state, False)

    attn_units(q_refs, 1, kv_ref, 0, stat_ref, acc_ref)


def attn_units(q_refs, half, kv_ref, part, stat_ref, acc_ref):
    keys, values_t = plane_rows(kv_ref, part, 0), plane_rows(kv_ref, part, 1).T
    for turn in range(2):
        for head in range(acc_ref.shape[1]):
            update_tile(q_refs, half, turn, head, keys, values_t, None, stat_ref.at[half], acc_ref.at[half], False)


def attn_remote_kernel(last, later_ref, *refs):
    q_refs, kv_ref = refs[:4], refs[4]
    outs = refs[-3:] if last else refs[-2:]
    stat_ref, acc_ref = outs[-2:]
    later = later_ref[0]
    attn_units(q_refs, later, kv_ref, later, stat_ref, acc_ref)
    attn_units(q_refs, 1, kv_ref, 0, stat_ref, acc_ref)
    if last:
        span = q_refs[0].shape[0] // 2
        for half in range(2):
            for head in range(acc_ref.shape[1]):
                scaled = acc_ref[half, head] / stat_ref[half, head, pl.ds(1, 1), :]
                outs[0][:, pl.ds(half * span, span), pl.ds(head * HEAD_SIZE, HEAD_SIZE)] = scaled.T.reshape(
                    4, span, HEAD_SIZE
                )


def pack(state, log_row):
    hi = lax.reduce_precision(log_row, 8, 7)
    mid = lax.reduce_precision(log_row - hi, 8, 7)
    row = lax.broadcasted_iota(jnp.int32, (16, state.shape[1]), 0)
    rest = jnp.where(row == 0, hi, jnp.where(row == 1, mid, jnp.where(row == 2, log_row - hi - mid, 0.0)))
    return jnp.concatenate([state.astype(BF16), rest.astype(BF16)], axis=0)


def unpack(packed):
    return packed[:NS].astype(F32), jnp.sum(packed[NS:].astype(F32), axis=0, keepdims=True)


def chain(first, second):
    return jnp.exp(second[1]) * first[0] + second[0], first[1] + second[1]


def split_body(
    queries,
    key_head_array,
    value_head_array,
    ssm_input,
    ssm_gate,
    ssm_write,
    ssm_read,
    step_size,
    log_decay,
    skip_gain,
    norm_gain,
    out_weight,
):
    planes = lax.axis_size("ctx") // 4
    ctx_index = lax.axis_index("ctx")
    tp_index = lax.axis_index("tp")
    z, y, core = ctx_index // 4, (ctx_index // 2) % 2, ctx_index % 2
    tok_dev = queries.shape[0]
    half = tok_dev // 2
    group = queries.shape[1] // 4
    everyone = range(4 * planes)
    to_core = [(i, i ^ 1) for i in everyone]
    to_y = [(i, i ^ 2) for i in everyone]

    def send(x, pairs):
        return lax.ppermute(x, "ctx", pairs)

    def part(x, which, width, axis):
        return lax.dynamic_slice_in_dim(x, which * width, width, axis)

    def in_order(mine, other, at, axis=0):
        return jnp.concatenate([jnp.where(at == 0, mine, other), jnp.where(at == 0, other, mine)], axis=axis)

    near = range(4)
    near_pairs = [None, to_core, to_y, [(i, i ^ 3) for i in everyone]]
    head_of = [2 * (core if k in (0, 2) else 1 - core) + (y if k < 2 else 1 - y) for k in near]

    def kv_piece(which):
        cut = [part(x, which, HEAD_SIZE, 1).reshape(2, half, HEAD_SIZE) for x in (key_head_array, value_head_array)]
        return jnp.stack(cut, axis=1)

    kv_near = {k: send(kv_piece(head_of[k]), near_pairs[k]) for k in (2, 3, 1)}
    kv_near[0] = kv_piece(head_of[0])
    kv_own = jnp.stack([kv_near[k] for k in near], axis=1)

    def across(by):
        return [(i, i ^ (4 * by)) for i in everyone]

    kv_from = {by: send(kv_own, across(by)) for by in range(1, planes)}

    q_mine, q_sent = part(queries, core, 2 * group, 1), part(queries, 1 - core, 2 * group, 1)
    q_other = send(q_sent, to_core)
    q_far = send(jnp.stack([part(q_mine, 1 - y, group, 1), part(q_other, 1 - y, group, 1)]), to_y)
    q_near = [part(q_mine, y, group, 1), part(q_other, y, group, 1), q_far[0], q_far[1]]

    groups = ssm_write.shape[1] // NS
    per_group = step_size.shape[0] // groups
    width = per_group * P_SIZE
    by_group = (groups, per_group, tok_dev)
    step_cols = jnp.transpose(step_size.reshape(by_group), (0, 2, 1))
    ld_rows = log_decay.reshape(by_group)
    ld_cols = jnp.transpose(ld_rows, (0, 2, 1))
    skip_rows = jnp.repeat(skip_gain, P_SIZE).reshape(groups, 1, width)
    gain_rows = norm_gain.reshape(groups, 1, width)
    wide = pl.BlockSpec((half, width), lambda b, g: (b, g))
    narrow = pl.BlockSpec((half, NS), lambda b, g: (b, g))
    columns = pl.BlockSpec((1, half, per_group), lambda b, g: (g, b, 0))
    per_row = pl.BlockSpec((1, 1, width), lambda b, g: (g, 0, 0))
    mixed, states = pl.pallas_call(
        ssm_local_kernel,
        grid=(2, groups),
        in_specs=[
            wide,
            narrow,
            narrow,
            columns,
            columns,
            pl.BlockSpec((1, per_group, half), lambda b, g: (g, 0, b)),
            per_row,
            pl.BlockSpec(memory_space=pl.ANY),
        ],
        out_specs=[wide, pl.BlockSpec((1, NS + 8, width), lambda b, g: (b, 0, g))],
        out_shape=[
            jax.ShapeDtypeStruct((tok_dev, groups * width), F32),
            jax.ShapeDtypeStruct((2, NS + 8, groups * width), F32),
        ],
        compiler_params=pltpu.CompilerParams(vmem_limit_bytes=32 * 2**20),
        cost_estimate=pl.CostEstimate(flops=4 * 10**8, bytes_accessed=6 * 2**20, transcendentals=10**6),
        name="ssm_local",
    )(ssm_input, ssm_write, ssm_read, step_cols, ld_cols, ld_rows, skip_rows, kv_near[1][0, 0, :16])

    st_mine = part(states, core, 2 * width, 2)
    st_other = send(part(states, 1 - core, 2 * width, 2), to_core)
    st_zero, st_one = jnp.where(core == 0, st_mine, st_other), jnp.where(core == 0, st_other, st_mine)

    def elem(packed):
        return packed[:NS], packed[NS : NS + 1]

    early_chip = chain(elem(st_zero[0]), elem(st_one[0]))
    late_chip = chain(elem(st_one[1]), elem(st_zero[1]))
    chip_pack = jnp.stack([pack(*early_chip), pack(*late_chip)])
    cp_mine = part(chip_pack, y, width, 2)
    cp_other = send(part(chip_pack, 1 - y, width, 2), to_y)
    cp_zero, cp_one = jnp.where(y == 0, cp_mine, cp_other), jnp.where(y == 0, cp_other, cp_mine)
    early_plane = chain(unpack(cp_zero[0]), unpack(cp_one[0]))
    late_plane = chain(unpack(cp_one[1]), unpack(cp_zero[1]))
    def ordered_pair(mine, other, low):
        first = jax.tree.map(lambda a, b: jnp.where(low, a, b), mine, other)
        second = jax.tree.map(lambda a, b: jnp.where(low, b, a), mine, other)
        return chain(first[0], second[0]), chain(second[1], first[1])

    zero = (jnp.zeros((NS, width), F32), jnp.zeros((1, width), F32))
    span_own = (early_plane, late_plane)
    before, after = zero, zero
    z_came = []
    for bit in range(planes.bit_length() - 1):
        low = (z >> bit) % 2 == 0
        span_pack = jnp.stack([pack(*span_own[0]), pack(*span_own[1])])
        came = send(span_pack, across(1 << bit))
        z_came.append(came)
        span_other = (unpack(came[0]), unpack(came[1]))
        before = jax.tree.map(lambda a, b: jnp.where(low, b, a), chain(span_other[0], before), before)
        after = jax.tree.map(lambda a, b: jnp.where(low, a, b), chain(span_other[1], after), after)
        span_own = ordered_pair(span_own, span_other, low)
    enter_early = before[0]
    enter_late = chain(span_own[0], after)[0]

    def step_on(state, packed):
        block = unpack(packed)
        return jnp.exp(block[1]) * state + block[0]

    early_at = [enter_early, step_on(enter_early, cp_zero[0])]
    late_at = [step_on(enter_late, cp_one[1]), enter_late]
    chip_enter = [jnp.stack([early_at[k], late_at[k]]).astype(BF16) for k in range(2)]
    ce_mine = jnp.where(y == 0, chip_enter[0], chip_enter[1])
    ce_other = send(jnp.where(y == 0, chip_enter[1], chip_enter[0]), to_y)
    ce = in_order(ce_mine, ce_other, y, axis=2).astype(F32)

    def step_by(state, block):
        return jnp.exp(block[1]) * state + block[0]

    early_block = [ce[0], step_by(ce[0], elem(st_zero[0]))]
    late_block = [step_by(ce[1], elem(st_one[1])), ce[1]]
    block_enter = [jnp.stack([early_block[k], late_block[k]]).astype(BF16) for k in range(2)]
    be_mine = jnp.where(core == 0, block_enter[0], block_enter[1])
    be_other = send(jnp.where(core == 0, block_enter[1], block_enter[0]), to_core)
    enter = in_order(be_mine, be_other, core, axis=2)

    ssm_output = pl.pallas_call(
        ssm_out_kernel,
        grid=(2, groups),
        in_specs=[
            wide,
            narrow,
            columns,
            pl.BlockSpec((1, NS, width), lambda b, g: (b, 0, g)),
            wide,
            per_row,
        ],
        out_specs=wide,
        out_shape=jax.ShapeDtypeStruct((tok_dev, groups * width), F32),
        compiler_params=pltpu.CompilerParams(vmem_limit_bytes=32 * 2**20),
        cost_estimate=pl.CostEstimate(flops=10**8, bytes_accessed=6 * 2**20, transcendentals=10**6),
        name="ssm_out",
    )(mixed, ssm_read, ld_cols, enter, ssm_gate, gain_rows)

    heads_own = group // HEAD_SIZE
    rows = 4 * half
    state_shapes = [
        jax.ShapeDtypeStruct((2, heads_own, 8, rows), F32),
        jax.ShapeDtypeStruct((2, heads_own, HEAD_SIZE, rows), F32),
    ]
    out_shape = jax.ShapeDtypeStruct((4, tok_dev, group), F32)
    params = pltpu.CompilerParams(vmem_limit_bytes=28 * 2**20)
    cost = pl.CostEstimate(flops=2 * 10**9, bytes_accessed=8 * 2**20, transcendentals=2 * 10**6)
    smem = pl.BlockSpec(memory_space=pltpu.SMEM)
    anywhere = pl.BlockSpec(memory_space=pl.ANY)

    def attend(kernel, name, scalars, kv, states, after, last=False):
        outs = ([out_shape] if last else []) + state_shapes
        return pl.pallas_call(
            kernel,
            in_specs=[smem] + [VMEM_SPEC] * (5 + len(states)) + [anywhere] * len(after),
            out_specs=[VMEM_SPEC] * len(outs),
            out_shape=outs,
            input_output_aliases={6 + k: len(outs) - 2 + k for k in range(len(states))},
            compiler_params=params,
            cost_estimate=cost,
            name=name,
        )(scalars, *q_near, kv, *states, *[x[0, :16, :128] for x in after])

    place = jnp.stack([y, core]).astype(jnp.int32)
    states = attend(attn_local_kernel, "attn_local", place, kv_own, [], [])
    for by in range(1, planes):
        last = by == planes - 1
        later = (z ^ by > z).astype(jnp.int32).reshape(1)
        waits = {1: [cp_other], 3: [z_came[0]]}.get(by, [])
        *result, stat, acc = attend(
            functools.partial(attn_remote_kernel, last), "attn_remote", later, kv_from[by], states, waits, last
        )
        states = [stat, acc]
    heads_plane = result[0].astype(BF16)

    pieces = [heads_plane[0]] + [send(heads_plane[k], near_pairs[k]) for k in (1, 2, 3)]
    attn_heads = in_order(
        in_order(pieces[0], pieces[2], y, axis=1), in_order(pieces[1], pieces[3], y, axis=1), core, axis=1
    )
    head_terms = jnp.dot(attn_heads, out_weight, preferred_element_type=F32)
    out_cols = out_weight.shape[1] // 2
    away = part(head_terms, 1 - tp_index, out_cols, 1).astype(BF16)
    came = lax.ppermute(away, "tp", [(0, 1), (1, 0)])
    attn_mixed = part(head_terms, tp_index, out_cols, 1) + came.astype(F32)
    return attn_mixed, ssm_output


def solution(mesh):
    placed = (
        P("ctx", "tp"),
        P("ctx", "tp"),
        P("ctx", "tp"),
        P("ctx", "tp"),
        P("ctx", "tp"),
        P("ctx", "tp"),
        P("ctx", "tp"),
        P("tp", "ctx"),
        P("tp", "ctx"),
        P("tp"),
        P("tp"),
        P("tp", None),
    )

    def program(*arrays):
        kv_dev, groups_dev = arrays[1].shape[1] // HEAD_SIZE, arrays[5].shape[1] // NS
        can_split = kv_dev == 4 and groups_dev == 4 and lax.axis_size("tp") == 2
        if can_split and lax.axis_size("ctx") in (8, 16, 32, 64):
            return split_body(*arrays)
        return body(*arrays)

    return jax.shard_map(
        program,
        mesh=mesh,
        in_specs=placed,
        out_specs=(P("ctx", "tp"), P("ctx", "tp")),
        check_vma=False,
    )
```

```python
import functools
import math

import jax
import jax.numpy as jnp
from jax import lax
from jax.experimental import pallas as pl
from jax.experimental.pallas import tpu as pltpu
from jax.sharding import PartitionSpec as P

HEAD_SIZE = 128
P_SIZE = 64
NS = 128


neg_big = -1e30


def prefix_2(x, axis, combine, identity, reverse):
    count, mine = (lax.axis_size(axis), lax.axis_index(axis))
    everything = jax.tree.map(lambda part: lax.all_gather(part, axis), x)
    start = jax.tree.map(
        lambda part, zero: jnp.broadcast_to(jnp.asarray(zero, part.dtype), part.shape), x, identity
    )

    def lap(k, before):
        at = count - 1 - k if reverse else k
        reached = at > mine if reverse else at < mine
        new = combine(before, jax.tree.map(lambda part: part[at], everything))
        return jax.tree.map(lambda a, b: jnp.where(reached, a, b), new, before)

    return lax.fori_loop(0, count, lap, start)


def broadcast(x, axis, root):
    mine = lax.axis_index(axis) == root
    return lax.psum(jnp.where(mine, x, jnp.zeros_like(x)), axis)


def online_update(running, query_blk, key_blk, value_blk, query_pos, key_pos, score_scale):
    top_old, total_old, acc_old = running
    scores = (
        jnp.einsum("qgrd,kgd->grqk", query_blk, key_blk, preferred_element_type=jnp.float32)
        * score_scale
    )
    allowed = key_pos[None, None, None, :] <= query_pos[None, None, :, None]
    top_block = jnp.max(jnp.where(allowed, scores, neg_big), axis=-1)
    top_new = jnp.maximum(top_old, top_block)
    weights = jnp.where(allowed, jnp.exp(scores - top_new[..., None]), 0.0)
    factor = jnp.exp(top_old - top_new)
    total_new = total_old * factor + jnp.sum(weights, axis=-1)
    acc_new = acc_old * factor[..., None] + jnp.einsum(
        "grqk,kgd->grqd",
        weights.astype(jnp.bfloat16),
        value_blk,
        preferred_element_type=jnp.float32,
    )
    return (top_new, total_new, acc_new)


def compose(earlier, later):
    return (earlier[0] * later[0], later[0][..., None, None] * earlier[1] + later[1])


def steps_for():
    return 4


def body(
    queries,
    key_head_array,
    value_head_array,
    ssm_input,
    ssm_gate,
    ssm_write,
    ssm_read,
    step_size,
    log_decay,
    skip_gain,
    norm_gain,
    out_weight,
):
    ctx_count = lax.axis_size("ctx")
    ctx_index = lax.axis_index("ctx")
    tok_dev = queries.shape[0]
    half = tok_dev // 2
    kv_dev = key_head_array.shape[1] // HEAD_SIZE
    heads_dev = queries.shape[1] // HEAD_SIZE
    group_repeat = heads_dev // kv_dev
    score_scale = 1.0 / math.sqrt(HEAD_SIZE)
    last_block = 2 * ctx_count - 1
    row_ids = jnp.arange(half, dtype=jnp.int32)
    early_qpos = ctx_index * half + row_ids
    late_qpos = (last_block - ctx_index) * half + row_ids
    query_early = queries[:half].reshape(half, kv_dev, group_repeat, HEAD_SIZE)
    query_late = queries[half:].reshape(half, kv_dev, group_repeat, HEAD_SIZE)

    def fresh_state():
        return (
            jnp.full((kv_dev, group_repeat, half), neg_big, jnp.float32),
            jnp.zeros((kv_dev, group_repeat, half), jnp.float32),
            jnp.zeros((kv_dev, group_repeat, half, HEAD_SIZE), jnp.float32),
        )

    key_piece = lax.all_gather(key_head_array, "ctx", axis=0, tiled=True)
    value_piece = lax.all_gather(value_head_array, "ctx", axis=0, tiled=True)
    shard_count = key_piece.shape[0] // tok_dev
    per_step = steps_for()
    turns = shard_count // per_step
    key_groups = key_piece.reshape(turns, per_step, 2, half, kv_dev, HEAD_SIZE)
    value_groups = value_piece.reshape(turns, per_step, 2, half, kv_dev, HEAD_SIZE)

    def one_turn(running_pair, inputs):
        key_grp, value_grp, turn_index = inputs
        base_shard = turn_index * per_step
        shard_ids = base_shard + jnp.arange(per_step, dtype=jnp.int32)
        early_kpos = (shard_ids[:, None] * half + row_ids[None, :]).reshape(-1)
        late_kpos = ((last_block - shard_ids)[:, None] * half + row_ids[None, :]).reshape(-1)
        early_keys = key_grp[:, 0].reshape(per_step * half, kv_dev, HEAD_SIZE)
        late_keys = key_grp[:, 1].reshape(per_step * half, kv_dev, HEAD_SIZE)
        early_vals = value_grp[:, 0].reshape(per_step * half, kv_dev, HEAD_SIZE)
        late_vals = value_grp[:, 1].reshape(per_step * half, kv_dev, HEAD_SIZE)
        run_early, run_late = running_pair
        run_early = lax.cond(
            base_shard <= ctx_index,
            lambda running_now: online_update(
                running_now,
                query_early,
                early_keys,
                early_vals,
                early_qpos,
                early_kpos,
                score_scale,
            ),
            lambda running_now: running_now,
            run_early,
        )
        run_late = online_update(
            run_late, query_late, early_keys, early_vals, late_qpos, early_kpos, score_scale
        )
        run_late = lax.cond(
            base_shard + per_step - 1 >= ctx_index,
            lambda running_now: online_update(
                running_now, query_late, late_keys, late_vals, late_qpos, late_kpos, score_scale
            ),
            lambda running_now: running_now,
            run_late,
        )
        return ((run_early, run_late), None)

    result_pair, unused_out = lax.scan(
        one_turn,
        (fresh_state(), fresh_state()),
        (key_groups, value_groups, jnp.arange(turns, dtype=jnp.int32)),
    )

    def finish(running):
        top_fin, total_fin, acc_fin = running
        heads_out = acc_fin / total_fin[..., None]
        return (
            jnp.transpose(heads_out, (2, 0, 1, 3))
            .reshape(half, heads_dev * HEAD_SIZE)
            .astype(jnp.bfloat16)
        )

    attn_heads = jnp.concatenate([finish(result_pair[0]), finish(result_pair[1])], axis=0)
    head_terms = jnp.dot(attn_heads, out_weight, preferred_element_type=jnp.float32)
    attn_mixed = lax.psum_scatter(head_terms, "tp", scatter_dimension=1, tiled=True)
    heads_ssm = step_size.shape[0]
    groups_dev = ssm_write.shape[1] // NS
    per_group = heads_ssm // groups_dev
    causal = row_ids[:, None] >= row_ids[None, :]
    skip_cols = skip_gain.reshape(groups_dev, per_group)
    gain_cols = norm_gain.reshape(groups_dev, per_group * P_SIZE)

    def block_parts(row_from):
        cum_decay = jnp.dot(
            log_decay[:, row_from : row_from + half],
            (row_ids[:, None] <= row_ids[None, :]).astype(jnp.float32),
            precision=lax.Precision.HIGHEST,
        ).reshape(groups_dev, per_group, half)
        step_blk = step_size[:, row_from : row_from + half].reshape(groups_dev, per_group, half)
        input_blk = ssm_input[row_from : row_from + half].reshape(
            half, groups_dev, per_group, P_SIZE
        )
        write_blk = ssm_write[row_from : row_from + half].reshape(half, groups_dev, NS)
        read_blk = ssm_read[row_from : row_from + half].reshape(half, groups_dev, NS)
        scaled = (
            input_blk.astype(jnp.float32) * jnp.transpose(step_blk, (2, 0, 1))[..., None]
        ).astype(jnp.bfloat16)
        inner_prod = jnp.einsum(
            "tgn,sgn->gts", read_blk, write_blk, preferred_element_type=jnp.float32
        )
        decay_gap = cum_decay[..., :, None] - cum_decay[..., None, :]
        mixing = jnp.where(
            causal, inner_prod[:, None] * jnp.exp(jnp.where(causal, decay_gap, 0.0)), 0.0
        ).astype(jnp.bfloat16)
        local_out = jnp.einsum(
            "gjts,sgjp->tgjp", mixing, scaled, preferred_element_type=jnp.float32
        )
        tail_decay = jnp.exp(cum_decay[..., -1:] - cum_decay)
        written = (
            jnp.transpose(write_blk, (1, 0, 2)).astype(jnp.float32)[:, None] * tail_decay[..., None]
        ).astype(jnp.bfloat16)
        block_state = jnp.einsum(
            "sgjp,gjsn->gjpn", scaled, written, preferred_element_type=jnp.float32
        )
        block_decay = jnp.exp(cum_decay[..., -1])
        return ((block_decay, block_state), (local_out, cum_decay, read_blk, input_blk, row_from))

    def block_output(entering, pieces):
        local_out, cum_decay, read_blk, input_blk, row_from = pieces
        carried = jnp.einsum(
            "tgn,gjpn->tgjp",
            read_blk.astype(jnp.float32),
            entering,
            precision=lax.Precision.HIGHEST,
        )
        mixed_out = (
            local_out
            + carried * jnp.transpose(jnp.exp(cum_decay), (2, 0, 1))[..., None]
            + skip_cols[None, :, :, None] * input_blk.astype(jnp.float32)
        )
        gate_blk = ssm_gate[row_from : row_from + half].reshape(
            half, groups_dev, per_group * P_SIZE
        )
        gated = mixed_out.reshape(half, groups_dev, per_group * P_SIZE) * jax.nn.silu(
            gate_blk.astype(jnp.float32)
        )
        mean_square = jnp.mean(gated * gated, axis=-1, keepdims=True)
        normed = gated * lax.rsqrt(mean_square + 1e-05) * gain_cols[None]
        return normed.reshape(half, heads_ssm * P_SIZE)

    early_elem, early_rest = block_parts(0)
    late_elem, late_rest = block_parts(half)
    unit_decay = jnp.ones((groups_dev, per_group), jnp.float32)
    zero_state = jnp.zeros((groups_dev, per_group, P_SIZE, NS), jnp.float32)
    prefix = prefix_2(
        (early_elem[0], early_elem[1]), "ctx", compose, (unit_decay, zero_state), False
    )
    inclusive = compose(prefix, early_elem)
    total_state = broadcast(inclusive[1], "ctx", ctx_count - 1)
    suffix = prefix_2((late_elem[0], late_elem[1]), "ctx", compose, (unit_decay, zero_state), True)
    late_entering = suffix[0][..., None, None] * total_state + suffix[1]
    ssm_output = jnp.concatenate(
        [block_output(prefix[1], early_rest), block_output(late_entering, late_rest)], axis=0
    )
    return (attn_mixed, ssm_output)


LOG2E = 1.4426950408889634
F32 = jnp.float32
BF16 = jnp.bfloat16
HIGH = lax.Precision.HIGHEST
NT = (((1,), (1,)), ((), ()))
TN = (((0,), (0,)), ((), ()))
VMEM_SPEC = pl.BlockSpec(memory_space=pltpu.VMEM)


def expand_pairs(cols, pair):
    rows = cols.shape[0]
    lane = lax.broadcasted_iota(jnp.int32, (rows, 2 * P_SIZE), 1)
    first, second = cols[:, 2 * pair : 2 * pair + 1], cols[:, 2 * pair + 1 : 2 * pair + 2]
    return jnp.where(lane < P_SIZE, first, second)


def ssm_local_kernel(x_ref, write_ref, read_ref, step_ref, ldc_ref, ldr_ref, skip_ref, _, mixed_ref, state_ref):
    span = x_ref.shape[0]
    per_group = step_ref.shape[2]
    row = lax.broadcasted_iota(jnp.int32, (span, span), 0)
    col = lax.broadcasted_iota(jnp.int32, (span, span), 1)
    causal = col <= row
    tri = causal.astype(F32)
    ldc, ldr, step = ldc_ref[0], ldr_ref[0], step_ref[0]
    cum_c = jnp.dot(tri, ldc, precision=HIGH, preferred_element_type=F32)
    cum_r = lax.dot_general(ldr, tri, NT, precision=HIGH, preferred_element_type=F32)
    write, read = write_ref[...], read_ref[...]
    inner = lax.dot_general(read, write, NT, preferred_element_type=F32)
    last = cum_c[span - 1 : span, :]
    tail = jnp.exp(last - cum_c)
    lane = lax.broadcasted_iota(jnp.int32, (span, 2 * P_SIZE), 1)
    weighted = []
    for pair in range(per_group // 2):
        cols = pl.ds(pair * 2 * P_SIZE, 2 * P_SIZE)
        x = x_ref[:, cols].astype(F32)
        scaled = (x * expand_pairs(step, pair)).astype(BF16)
        mixes = []
        for head in (2 * pair, 2 * pair + 1):
            gap = cum_c[:, head : head + 1] - cum_r[head : head + 1, :]
            decay = jnp.exp(jnp.where(causal, gap, 0.0))
            mixes.append(jnp.where(causal, inner * decay, 0.0).astype(BF16))
        zero = jnp.zeros_like(scaled)
        stacked = jnp.concatenate(
            [jnp.where(lane < P_SIZE, scaled, zero), jnp.where(lane >= P_SIZE, scaled, zero)], axis=0
        )
        local = jnp.dot(jnp.concatenate(mixes, axis=1), stacked, preferred_element_type=F32)
        mixed_ref[:, cols] = local + skip_ref[0, :, cols] * x
        weighted.append((scaled.astype(F32) * expand_pairs(tail, pair)).astype(BF16))
        state_ref[0, pl.ds(NS, 8), cols] = jnp.broadcast_to(expand_pairs(last, pair), (8, 2 * P_SIZE))
    state_ref[0, pl.ds(0, NS), :] = lax.dot_general(
        write, jnp.concatenate(weighted, axis=1), TN, preferred_element_type=F32
    )


def ssm_out_kernel(mixed_ref, read_ref, ldc_ref, enter_ref, gate_ref, gain_ref, out_ref):
    span = mixed_ref.shape[0]
    row = lax.broadcasted_iota(jnp.int32, (span, span), 0)
    col = lax.broadcasted_iota(jnp.int32, (span, span), 1)
    tri = (col <= row).astype(F32)
    cum_c = jnp.dot(tri, ldc_ref[0], precision=HIGH, preferred_element_type=F32)
    grow = jnp.exp(cum_c)
    carried = jnp.dot(read_ref[...], enter_ref[0], preferred_element_type=F32)
    grown = jnp.concatenate([expand_pairs(grow, pair) for pair in range(grow.shape[1] // 2)], axis=1)
    gate = gate_ref[...].astype(F32)
    gated = (mixed_ref[...] + carried * grown) * (gate / (1.0 + jnp.exp(-gate)))
    mean_square = jnp.mean(gated * gated, axis=1, keepdims=True)
    out_ref[...] = gated * lax.rsqrt(mean_square + 1e-05) * gain_ref[0]


def attend_tile(q, keys, values_t, running, allowed):
    m_old, l_old, acc_old = running
    c = LOG2E / math.sqrt(HEAD_SIZE)
    s = lax.dot_general(keys, q, NT, preferred_element_type=F32)
    if allowed is not None:
        s = jnp.where(allowed, s, neg_big)
    m_new = jnp.max(s, axis=0, keepdims=True)
    if m_old is not None:
        m_new = jnp.maximum(m_old, m_new)
    p = jnp.exp2((s - m_new) * c)
    l_new = jnp.sum(p, axis=0, keepdims=True)
    acc_new = jnp.dot(values_t, p.astype(BF16), preferred_element_type=F32)
    if m_old is not None:
        alpha = jnp.exp2((m_old - m_new) * c)
        l_new = l_new + alpha * l_old
        acc_new = acc_new + alpha * acc_old
    return m_new, l_new, acc_new


def plane_rows(ref, half, which):
    chunk = ref[:, which] if half is None else ref[half, :, which]
    return chunk.reshape(-1, HEAD_SIZE)


def update_tile(q_refs, half, turn, head, keys, values_t, allowed, stat_ref, acc_ref, first):
    span = q_refs[0].shape[0] // 2
    q = jnp.concatenate(
        [
            ref[pl.ds(half * span, span), pl.ds(head * HEAD_SIZE, HEAD_SIZE)]
            for ref in q_refs[2 * turn : 2 * turn + 2]
        ],
        axis=0,
    )
    where = pl.ds(turn * 2 * span, 2 * span)
    running = (None, None, None)
    if not first:
        running = (stat_ref[head, pl.ds(0, 1), where], stat_ref[head, pl.ds(1, 1), where], acc_ref[head, :, where])
    running = attend_tile(q, keys, values_t, running, allowed)
    stat_ref[head, pl.ds(0, 1), where] = running[0]
    stat_ref[head, pl.ds(1, 1), where] = running[1]
    acc_ref[head, :, where] = running[2]


def attn_local_kernel(place_ref, *refs):
    q_refs, kv_ref, (stat_ref, acc_ref) = refs[:4], refs[4], refs[-2:]
    y, core = place_ref[0], place_ref[1]
    span = q_refs[0].shape[0] // 2
    heads = q_refs[0].shape[1] // HEAD_SIZE
    tile = 2 * span

    def position(shape, dim, half):
        at = lax.broadcasted_iota(jnp.int32, shape, dim)
        block = jnp.where(at < span, core, 1 - core)
        return (block if half == 0 else 1 - block) * span + at % span

    for half in range(2):
        state = stat_ref.at[half], acc_ref.at[half]
        allowed = position((tile, 1), 0, half) <= position((1, tile), 1, half)
        parts = []
        for turn in range(2):
            keys = kv_ref[half, 2 * turn : 2 * turn + 2, 0].reshape(tile, HEAD_SIZE)
            values_t = kv_ref[half, 2 * turn : 2 * turn + 2, 1].reshape(tile, HEAD_SIZE).T
            parts.append((keys, values_t))
            for head in range(heads):
                update_tile(q_refs, half, turn, head, keys, values_t, allowed, *state, True)
        for turn in range(2):

            @pl.when(y == (1 - turn if half == 0 else turn))
            def _():
                for head in range(heads):
                    update_tile(q_refs, half, turn, head, *parts[1 - turn], None, *state, False)

    attn_units(q_refs, 1, kv_ref, 0, stat_ref, acc_ref)


def attn_units(q_refs, half, kv_ref, part, stat_ref, acc_ref):
    keys, values_t = plane_rows(kv_ref, part, 0), plane_rows(kv_ref, part, 1).T
    for turn in range(2):
        for head in range(acc_ref.shape[1]):
            update_tile(q_refs, half, turn, head, keys, values_t, None, stat_ref.at[half], acc_ref.at[half], False)


def attn_remote_kernel(last, later_ref, *refs):
    q_refs, kv_ref = refs[:4], refs[4]
    outs = refs[-3:] if last else refs[-2:]
    stat_ref, acc_ref = outs[-2:]
    later = later_ref[0]
    attn_units(q_refs, later, kv_ref, later, stat_ref, acc_ref)
    attn_units(q_refs, 1, kv_ref, 0, stat_ref, acc_ref)
    if last:
        span = q_refs[0].shape[0] // 2
        for half in range(2):
            for head in range(acc_ref.shape[1]):
                scaled = acc_ref[half, head] / stat_ref[half, head, pl.ds(1, 1), :]
                outs[0][:, pl.ds(half * span, span), pl.ds(head * HEAD_SIZE, HEAD_SIZE)] = scaled.T.reshape(
                    4, span, HEAD_SIZE
                )


def pack(state, log_row):
    hi = lax.reduce_precision(log_row, 8, 7)
    mid = lax.reduce_precision(log_row - hi, 8, 7)
    row = lax.broadcasted_iota(jnp.int32, (16, state.shape[1]), 0)
    rest = jnp.where(row == 0, hi, jnp.where(row == 1, mid, jnp.where(row == 2, log_row - hi - mid, 0.0)))
    return jnp.concatenate([state.astype(BF16), rest.astype(BF16)], axis=0)


def unpack(packed):
    return packed[:NS].astype(F32), jnp.sum(packed[NS:].astype(F32), axis=0, keepdims=True)


def chain(first, second):
    return jnp.exp(second[1]) * first[0] + second[0], first[1] + second[1]


def split_body(
    queries,
    key_head_array,
    value_head_array,
    ssm_input,
    ssm_gate,
    ssm_write,
    ssm_read,
    step_size,
    log_decay,
    skip_gain,
    norm_gain,
    out_weight,
):
    planes = lax.axis_size("ctx") // 4
    ctx_index = lax.axis_index("ctx")
    tp_index = lax.axis_index("tp")
    z, y, core = ctx_index // 4, (ctx_index // 2) % 2, ctx_index % 2
    tok_dev = queries.shape[0]
    half = tok_dev // 2
    group = queries.shape[1] // 4
    everyone = range(4 * planes)
    to_core = [(i, i ^ 1) for i in everyone]
    to_y = [(i, i ^ 2) for i in everyone]

    def send(x, pairs):
        return lax.ppermute(x, "ctx", pairs)

    def part(x, which, width, axis):
        return lax.dynamic_slice_in_dim(x, which * width, width, axis)

    def in_order(mine, other, at, axis=0):
        return jnp.concatenate([jnp.where(at == 0, mine, other), jnp.where(at == 0, other, mine)], axis=axis)

    near = range(4)
    near_pairs = [None, to_core, to_y, [(i, i ^ 3) for i in everyone]]
    head_of = [2 * (core if k in (0, 2) else 1 - core) + (y if k < 2 else 1 - y) for k in near]

    def kv_piece(which):
        cut = [part(x, which, HEAD_SIZE, 1).reshape(2, half, HEAD_SIZE) for x in (key_head_array, value_head_array)]
        return jnp.stack(cut, axis=1)

    kv_near = {k: send(kv_piece(head_of[k]), near_pairs[k]) for k in (2, 3, 1)}
    kv_near[0] = kv_piece(head_of[0])
    kv_own = jnp.stack([kv_near[k] for k in near], axis=1)

    def across(by):
        return [(i, i ^ (4 * by)) for i in everyone]

    kv_from = {by: send(kv_own, across(by)) for by in range(1, planes)}

    q_mine, q_sent = part(queries, core, 2 * group, 1), part(queries, 1 - core, 2 * group, 1)
    q_other = send(q_sent, to_core)
    q_far = send(jnp.stack([part(q_mine, 1 - y, group, 1), part(q_other, 1 - y, group, 1)]), to_y)
    q_near = [part(q_mine, y, group, 1), part(q_other, y, group, 1), q_far[0], q_far[1]]

    groups = ssm_write.shape[1] // NS
    per_group = step_size.shape[0] // groups
    width = per_group * P_SIZE
    by_group = (groups, per_group, tok_dev)
    step_cols = jnp.transpose(step_size.reshape(by_group), (0, 2, 1))
    ld_rows = log_decay.reshape(by_group)
    ld_cols = jnp.transpose(ld_rows, (0, 2, 1))
    skip_rows = jnp.repeat(skip_gain, P_SIZE).reshape(groups, 1, width)
    gain_rows = norm_gain.reshape(groups, 1, width)
    wide = pl.BlockSpec((half, width), lambda b, g: (b, g))
    narrow = pl.BlockSpec((half, NS), lambda b, g: (b, g))
    columns = pl.BlockSpec((1, half, per_group), lambda b, g: (g, b, 0))
    per_row = pl.BlockSpec((1, 1, width), lambda b, g: (g, 0, 0))
    mixed, states = pl.pallas_call(
        ssm_local_kernel,
        grid=(2, groups),
        in_specs=[
            wide,
            narrow,
            narrow,
            columns,
            columns,
            pl.BlockSpec((1, per_group, half), lambda b, g: (g, 0, b)),
            per_row,
            pl.BlockSpec(memory_space=pl.ANY),
        ],
        out_specs=[wide, pl.BlockSpec((1, NS + 8, width), lambda b, g: (b, 0, g))],
        out_shape=[
            jax.ShapeDtypeStruct((tok_dev, groups * width), F32),
            jax.ShapeDtypeStruct((2, NS + 8, groups * width), F32),
        ],
        compiler_params=pltpu.CompilerParams(vmem_limit_bytes=32 * 2**20),
        cost_estimate=pl.CostEstimate(flops=4 * 10**8, bytes_accessed=6 * 2**20, transcendentals=10**6),
        name="ssm_local",
    )(ssm_input, ssm_write, ssm_read, step_cols, ld_cols, ld_rows, skip_rows, kv_near[1][0, 0, :16])

    st_mine = part(states, core, 2 * width, 2)
    st_other = send(part(states, 1 - core, 2 * width, 2), to_core)
    st_zero, st_one = jnp.where(core == 0, st_mine, st_other), jnp.where(core == 0, st_other, st_mine)

    def elem(packed):
        return packed[:NS], packed[NS : NS + 1]

    early_chip = chain(elem(st_zero[0]), elem(st_one[0]))
    late_chip = chain(elem(st_one[1]), elem(st_zero[1]))
    chip_pack = jnp.stack([pack(*early_chip), pack(*late_chip)])
    cp_mine = part(chip_pack, y, width, 2)
    cp_other = send(part(chip_pack, 1 - y, width, 2), to_y)
    cp_zero, cp_one = jnp.where(y == 0, cp_mine, cp_other), jnp.where(y == 0, cp_other, cp_mine)
    early_plane = chain(unpack(cp_zero[0]), unpack(cp_one[0]))
    late_plane = chain(unpack(cp_one[1]), unpack(cp_zero[1]))
    def ordered_pair(mine, other, low):
        first = jax.tree.map(lambda a, b: jnp.where(low, a, b), mine, other)
        second = jax.tree.map(lambda a, b: jnp.where(low, b, a), mine, other)
        return chain(first[0], second[0]), chain(second[1], first[1])

    zero = (jnp.zeros((NS, width), F32), jnp.zeros((1, width), F32))
    span_own = (early_plane, late_plane)
    before, after = zero, zero
    z_came = []
    for bit in range(planes.bit_length() - 1):
        low = (z >> bit) % 2 == 0
        span_pack = jnp.stack([pack(*span_own[0]), pack(*span_own[1])])
        came = send(span_pack, across(1 << bit))
        z_came.append(came)
        span_other = (unpack(came[0]), unpack(came[1]))
        before = jax.tree.map(lambda a, b: jnp.where(low, b, a), chain(span_other[0], before), before)
        after = jax.tree.map(lambda a, b: jnp.where(low, a, b), chain(span_other[1], after), after)
        span_own = ordered_pair(span_own, span_other, low)
    enter_early = before[0]
    enter_late = chain(span_own[0], after)[0]

    def step_on(state, packed):
        block = unpack(packed)
        return jnp.exp(block[1]) * state + block[0]

    early_at = [enter_early, step_on(enter_early, cp_zero[0])]
    late_at = [step_on(enter_late, cp_one[1]), enter_late]
    chip_enter = [jnp.stack([early_at[k], late_at[k]]).astype(BF16) for k in range(2)]
    ce_mine = jnp.where(y == 0, chip_enter[0], chip_enter[1])
    ce_other = send(jnp.where(y == 0, chip_enter[1], chip_enter[0]), to_y)
    ce = in_order(ce_mine, ce_other, y, axis=2).astype(F32)

    def step_by(state, block):
        return jnp.exp(block[1]) * state + block[0]

    early_block = [ce[0], step_by(ce[0], elem(st_zero[0]))]
    late_block = [step_by(ce[1], elem(st_one[1])), ce[1]]
    block_enter = [jnp.stack([early_block[k], late_block[k]]).astype(BF16) for k in range(2)]
    be_mine = jnp.where(core == 0, block_enter[0], block_enter[1])
    be_other = send(jnp.where(core == 0, block_enter[1], block_enter[0]), to_core)
    enter = in_order(be_mine, be_other, core, axis=2)

    ssm_output = pl.pallas_call(
        ssm_out_kernel,
        grid=(2, groups),
        in_specs=[
            wide,
            narrow,
            columns,
            pl.BlockSpec((1, NS, width), lambda b, g: (b, 0, g)),
            wide,
            per_row,
        ],
        out_specs=wide,
        out_shape=jax.ShapeDtypeStruct((tok_dev, groups * width), F32),
        compiler_params=pltpu.CompilerParams(vmem_limit_bytes=32 * 2**20),
        cost_estimate=pl.CostEstimate(flops=10**8, bytes_accessed=6 * 2**20, transcendentals=10**6),
        name="ssm_out",
    )(mixed, ssm_read, ld_cols, enter, ssm_gate, gain_rows)

    heads_own = group // HEAD_SIZE
    rows = 4 * half
    state_shapes = [
        jax.ShapeDtypeStruct((2, heads_own, 8, rows), F32),
        jax.ShapeDtypeStruct((2, heads_own, HEAD_SIZE, rows), F32),
    ]
    out_shape = jax.ShapeDtypeStruct((4, tok_dev, group), F32)
    params = pltpu.CompilerParams(vmem_limit_bytes=28 * 2**20)
    cost = pl.CostEstimate(flops=2 * 10**9, bytes_accessed=8 * 2**20, transcendentals=2 * 10**6)
    smem = pl.BlockSpec(memory_space=pltpu.SMEM)
    anywhere = pl.BlockSpec(memory_space=pl.ANY)

    def attend(kernel, name, scalars, kv, states, after, last=False):
        outs = ([out_shape] if last else []) + state_shapes
        return pl.pallas_call(
            kernel,
            in_specs=[smem] + [VMEM_SPEC] * (5 + len(states)) + [anywhere] * len(after),
            out_specs=[VMEM_SPEC] * len(outs),
            out_shape=outs,
            input_output_aliases={6 + k: len(outs) - 2 + k for k in range(len(states))},
            compiler_params=params,
            cost_estimate=cost,
            name=name,
        )(scalars, *q_near, kv, *states, *[x[0, :16, :128] for x in after])

    place = jnp.stack([y, core]).astype(jnp.int32)
    states = attend(attn_local_kernel, "attn_local", place, kv_own, [], [])
    for by in range(1, planes):
        last = by == planes - 1
        later = (z ^ by > z).astype(jnp.int32).reshape(1)
        waits = {1: [cp_other], 3: [z_came[0]]}.get(by, [])
        *result, stat, acc = attend(
            functools.partial(attn_remote_kernel, last), "attn_remote", later, kv_from[by], states, waits, last
        )
        states = [stat, acc]
    heads_plane = (result[0] + z_came[-1][0, -1, :1].astype(F32)).astype(BF16)

    pieces = [heads_plane[0]] + [send(heads_plane[k], near_pairs[k]) for k in (1, 2, 3)]
    attn_heads = in_order(
        in_order(pieces[0], pieces[2], y, axis=1), in_order(pieces[1], pieces[3], y, axis=1), core, axis=1
    )
    out_cols = out_weight.shape[1] // 2
    away = jnp.dot(attn_heads, part(out_weight, 1 - tp_index, out_cols, 1), preferred_element_type=F32)
    came = lax.ppermute(away.astype(BF16), "tp", [(0, 1), (1, 0)])
    mine = jnp.dot(attn_heads, part(out_weight, tp_index, out_cols, 1), preferred_element_type=F32)
    attn_mixed = lax.optimization_barrier(mine) + came.astype(F32)
    return attn_mixed, ssm_output


def solution(mesh):
    placed = (
        P("ctx", "tp"),
        P("ctx", "tp"),
        P("ctx", "tp"),
        P("ctx", "tp"),
        P("ctx", "tp"),
        P("ctx", "tp"),
        P("ctx", "tp"),
        P("tp", "ctx"),
        P("tp", "ctx"),
        P("tp"),
        P("tp"),
        P("tp", None),
    )

    def program(*arrays):
        kv_dev, groups_dev = arrays[1].shape[1] // HEAD_SIZE, arrays[5].shape[1] // NS
        can_split = kv_dev == 4 and groups_dev == 4 and lax.axis_size("tp") == 2
        if can_split and lax.axis_size("ctx") in (8, 16, 32, 64):
            return split_body(*arrays)
        return body(*arrays)

    return jax.shard_map(
        program,
        mesh=mesh,
        in_specs=placed,
        out_specs=(P("ctx", "tp"), P("ctx", "tp")),
        check_vma=False,
    )
```
